256 devices in a mesh: list: 64 (over y, z, core), sub: 4 (over x).
Axes of the slice: x: 4, y: 4, z: 8, core: 2. Of those that a mesh axis runs over, the one named last changes fastest.
Arguments:
- embeddings: bfloat16 [65536, 1280], P(('list', 'sub')), may hold values from -54 to 54
- coarse_list_index: int32 [65536], P(('list', 'sub')), may hold values from 0 to 65535, as said below
- slots: int32 [65536], P(('list', 'sub')), may hold values from 0 to 7, as said below
- codes: int32 [65536, 128], P(('list', 'sub')), may hold values from 0 to 255
- centroids: bfloat16 [65536, 1280], P('list'), may hold values from -6 to 6
- rotation: bfloat16 [1280, 1280], P(None, 'sub'), may hold values from -0.15625 to 0.15625
- old_codebook: float32 [256, 1280], P('list', 'sub'), may hold values from -6 to 6
Outputs:
- list_store: bfloat16 [131072, 1280], P('list', 'sub')
- codebook: float32 [256, 1280], P('list', 'sub')
The draws below stay inside these ranges and needn't reach their ends.
Inputs may be any that keep to these rules, and one draw needn't show every extreme that they name: `coarse_list_index`: the owner of list i is i // 1024. Rows of one device with the same owner have distinct slots; for a quarter of the owners every device fills all 8 slots.
All inputs are finite; a program needn't handle non-finite values.
Results may differ from the reference program's by a relative error of at most 0.005.
Values may be sent and summed in bfloat16 or wider, within the bound.
A program may use at most 64 MiB of HBM per device.

```python
import math
import jax
import jax.numpy as jnp
from jax import lax

D = 1280
DSUB = 10
CENT = 256
LIST_DEV = 1024
ROW_DEV = 256
SUBS = 128
OWNERS = 64
SUBSPACE_GROUPS = 4
LISTS = 65536
CAP = 8
SLOTS = 2048
ROWS = 65536
ANCHOR = 64


def routing(key):
    rank = jax.random.permutation(jax.random.fold_in(key, 101), OWNERS)
    hot_owner = rank < OWNERS // 4
    pool = OWNERS * CAP
    entry = jnp.arange(pool, dtype=jnp.int32)
    coldness = jnp.where(hot_owner[entry // CAP], 0, 1).astype(jnp.int32)

    def one_block(block_key):
        order_vals = jax.random.permutation(block_key, pool).astype(jnp.int32)
        score = coldness * pool + order_vals
        chosen = jnp.argsort(score)[:ROW_DEV].astype(jnp.int32)
        mixing = jax.random.permutation(jax.random.fold_in(block_key, 7), ROW_DEV)
        chosen = chosen[mixing]
        slot_vals = chosen % CAP
        local = jax.random.randint(jax.random.fold_in(block_key, 9), (ROW_DEV,), 0, LIST_DEV, dtype=jnp.int32)
        local = jnp.where(slot_vals == 0, 0, local)
        local = jnp.where(slot_vals == CAP - 1, LIST_DEV - 1, local)
        return (chosen // CAP * LIST_DEV + local, slot_vals)
    block_keys = jax.random.split(jax.random.fold_in(key, 202), ROWS // ROW_DEV)
    ids_all, slot_all = jax.vmap(one_block)(block_keys)
    return (ids_all.reshape(ROWS), slot_all.reshape(ROWS))


def draw_coarse_list_index(key, part):
    ids_all, slot_all = routing(key)
    return ids_all


def draw_slots(key, part):
    ids_all, slot_all = routing(key)
    return slot_all


def draw_embeddings(key, part):
    key = jax.random.fold_in(key, 5)
    base_key, row_key, col_key = jax.random.split(key, 3)
    low = math.log(0.3)
    high = math.log(3.0)
    row_scale = jnp.exp(jax.random.uniform(row_key, (ROWS, 1), jnp.float32, low, high))
    col_scale = jnp.exp(jax.random.uniform(col_key, (1, D), jnp.float32, low, high))
    base = jnp.clip(jax.random.normal(base_key, (ROWS, D), jnp.float32), -6.0, 6.0)
    values = base * row_scale * col_scale
    return values.astype(jnp.bfloat16)


def touch_ends(values, key, least, high):
    longest = values.shape.index(max(values.shape))
    spots = []
    for shift in (0, 1):
        where = [jax.random.randint(jax.random.fold_in(key, axis), (), 0, length) for axis, length in enumerate(values.shape)]
        where[longest] = (where[longest] + shift) % values.shape[longest]
        spots.append(tuple(where))
    return values.at[spots[0]].set(least).at[spots[1]].set(high)


def block_levels(rng, shape, shards, smallest, high):
    def one(dim, blocks):
        heights = jax.random.uniform(jax.random.fold_in(jax.random.fold_in(rng, 6), dim), (blocks,), jnp.float32, smallest / len(shards), high / len(shards))
        return jnp.repeat(jnp.exp(heights), shape[dim] // blocks).reshape((-1,) + (1,) * (len(shape) - dim - 1))

    gain = one(*shards[0])
    for cut in shards[1:]:
        gain = gain * one(*cut)
    return gain


def bell_draw(stream_key, dims, deviation, most, pieces=(), kind=jnp.bfloat16):
    factor_of = block_levels(stream_key, dims, pieces, -0.22, 0.18) if pieces else 1.0
    result = jax.random.normal(stream_key, dims, jnp.float32) * deviation * factor_of
    return jnp.minimum(jnp.maximum(result, -most), most).astype(kind)


def setup_inputs(seed: int = 0) -> dict:
    keys = jax.random.split(jax.random.key(seed), 8)
    return {
        "embeddings": draw_embeddings(jax.random.fold_in(keys[7], 71), 0),
        "coarse_list_index": draw_coarse_list_index(jax.random.fold_in(keys[7], 71), 0),
        "slots": draw_slots(jax.random.fold_in(keys[7], 71), 0),
        "codes": touch_ends(jax.random.randint(keys[3], (ROWS, SUBS), 0, CENT), jax.random.fold_in(keys[3], 1), 0, CENT - 1).astype(jnp.int32),
        "centroids": bell_draw(keys[4], (LISTS, D), 1.0, 6.0, ((0, 64),)),
        "rotation": bell_draw(keys[5], (D, D), D ** -0.5, 0.15625, ((1, 4),)),
        "old_codebook": bell_draw(keys[6], (CENT, D), 1.0, 6.0, ((0, 64), (1, 4)), jnp.float32),
    }


def reference(embeddings, coarse_list_index, slots, codes, centroids, rotation, old_codebook):
    blocks = ROWS // ROW_DEV

    def one_block(carry, index):
        sums, counts = carry
        start = (index * ROW_DEV).astype(jnp.int32)
        rows_x = lax.dynamic_slice_in_dim(embeddings, start, ROW_DEV, 0)
        ids_x = lax.dynamic_slice_in_dim(coarse_list_index, start, ROW_DEV, 0)
        codes_x = lax.dynamic_slice_in_dim(codes, start, ROW_DEV, 0)
        centroid_row_vectors = jnp.take(centroids, ids_x, axis=0)
        residual = (rows_x.astype(jnp.float32) - centroid_row_vectors.astype(jnp.float32)).astype(jnp.bfloat16)
        rotated = jnp.dot(residual, rotation, preferred_element_type=jnp.float32).astype(jnp.bfloat16)
        segment = (jnp.arange(SUBS, dtype=jnp.int32)[None, :] * CENT + codes_x).reshape(-1)
        values_flat = rotated.astype(jnp.float32).reshape(ROW_DEV * SUBS, DSUB)
        sums = sums + jax.ops.segment_sum(values_flat, segment, num_segments=SUBS * CENT)
        counts = counts + jax.ops.segment_sum(jnp.ones((ROW_DEV * SUBS,), jnp.float32), segment, num_segments=SUBS * CENT)
        return (sums, counts), rotated

    init = (jnp.zeros((SUBS * CENT, DSUB), jnp.float32), jnp.zeros((SUBS * CENT,), jnp.float32))
    (sums, counts), rotated = lax.scan(one_block, init, jnp.arange(blocks, dtype=jnp.int32))
    row_index = jnp.arange(ROWS, dtype=jnp.int32)
    block = row_index // ROW_DEV
    owner = coarse_list_index // LIST_DEV
    position = ((owner * SUBSPACE_GROUPS + block % SUBSPACE_GROUPS) * OWNERS + block // SUBSPACE_GROUPS) * CAP + slots
    list_store = jnp.zeros((OWNERS * SLOTS, D), jnp.bfloat16).at[position].set(rotated.reshape(ROWS, D))
    sums = sums.reshape(SUBS, CENT, DSUB).transpose(1, 0, 2).reshape(CENT, D)
    counts = jnp.repeat(counts.reshape(SUBS, CENT).T, DSUB, axis=1)
    codebook = (sums + ANCHOR * old_codebook) / (counts + ANCHOR)
    return list_store, codebook
```

```python
import functools

import jax
import jax.numpy as jnp
import numpy as np
from jax import lax
from jax.experimental import pallas as pl
from jax.experimental.pallas import tpu as pltpu
from jax.sharding import PartitionSpec as P

MESH = pl.DeviceIdType.MESH
NY, NZ, NC, NX = 4, 8, 2, 4
OWNERS = NY * NZ * NC
ROW_DEV = 256
CAP = 8
D = 1280
HALF = D // 2
COLS = D // NX
CENT = 256
LIST_DEV = 1024
SUBS_DEV = 32
DSUB = 10
GROUPS = 4
CHIPS_G = 8
CHIPS = NY * NZ
ROWS_G = CHIPS_G * NC * CAP
MW = D + 256
PW = 384
PAY = COLS + SUBS_DEV
NT = (((1,), (1,)), ((), ()))
LANES = 128
SPLIT = (11, 11, 10)
FIRST = (0, 11, 22)
ANCHOR = 64.0
BF = jnp.bfloat16
F32 = jnp.float32


def layout_tables():
    spread = np.zeros((2 * PW, PAY), np.float32)
    back = np.zeros((2, len(SPLIT), LANES, COLS), np.float32)
    for g, (first, many) in enumerate(zip(FIRST, SPLIT)):
        for i in range(many):
            m = first + i
            for d in range(DSUB + 1):
                lane = i * (DSUB + 1) + d
                spread[PW + g * LANES + lane, COLS + m] = 1
                if d < DSUB:
                    spread[g * LANES + lane, m * DSUB + d] = 1
                    back[0, g, lane, m * DSUB + d] = 1
                    back[1, g, i * (DSUB + 1) + DSUB, m * DSUB + d] = 1
    return spread, back


def kernel(
    emb_hbm,
    idx_hbm,
    slot_hbm,
    codes_hbm,
    cent_hbm,
    rot_hbm,
    old_hbm,
    spread_hbm,
    back_hbm,
    store_hbm,
    book_ref,
    emb,
    idx,
    slot,
    codes,
    cent,
    rot,
    old,
    spread,
    back,
    outb,
    inb,
    res,
    pay_out,
    pay_in,
    hot,
    vals,
    acc,
    sum_out,
    sum_pair,
    sum_mid,
    sum_in,
    load_sem,
    swap_send,
    swap_recv,
    out_sem,
    in_sem,
    rot_send,
    rot_recv,
    pay_send,
    pay_recv,
    own_sem,
    pair_send,
    pair_recv,
    sum_send,
    sum_recv,
    store_sem,
):
    me = lax.axis_index("list")
    x = lax.axis_index("sub")
    core = lax.rem(me, NC)
    chip = me // NC
    z = lax.rem(chip, NZ)
    y = chip // NZ
    sibling = me + 1 - 2 * core
    right, left = lax.rem(x + 1, NX), lax.rem(x + NX - 1, NX)
    across = lax.rem(x + 2, NX)

    sources = [(emb_hbm, emb), (idx_hbm, idx), (slot_hbm, slot), (codes_hbm, codes)]
    loads = [
        pltpu.make_async_copy(src, dst.at[core], load_sem.at[i])
        for i, (src, dst) in enumerate(sources)
    ]
    later = [(cent_hbm, cent), (rot_hbm, rot.at[x]), (spread_hbm, spread), (back_hbm, back)]
    later.append((old_hbm, old))
    loads += [
        pltpu.make_async_copy(src, dst, load_sem.at[4 + i]) for i, (src, dst) in enumerate(later)
    ]
    for load in loads:
        load.start()

    barrier = pltpu.get_barrier_semaphore()

    def peer_of(k):
        return lax.rem(chip + k, CHIPS) * NC + core

    def greet(k, carry):
        pl.semaphore_signal(barrier, inc=1, device_id=(peer_of(k), x), device_id_type=MESH)
        return carry

    lax.fori_loop(1, CHIPS, greet, 0)
    pl.semaphore_signal(barrier, inc=1, device_id=(sibling, x), device_id_type=MESH)
    for k in range(1, NX):
        pl.semaphore_signal(
            barrier, inc=1, device_id=(me, lax.rem(x + k, NX)), device_id_type=MESH
        )
    pl.semaphore_wait(barrier, CHIPS + NX - 1)

    swaps = [
        pltpu.make_async_remote_copy(
            src_ref=src,
            dst_ref=dst.at[core],
            send_sem=swap_send.at[i],
            recv_sem=swap_recv.at[i],
            device_id=(sibling, x),
            device_id_type=MESH,
        )
        for i, (src, dst) in enumerate(sources)
    ]
    for swap in swaps:
        swap.start()

    half = COLS // 2
    half_rows = pl.ds(pl.multiple_of(core * half, half), half)
    quarter_a = pl.ds(pl.multiple_of(core * half, half // 2), half // 2)
    quarter_b = pl.ds(pl.multiple_of(core * half + half // 2, half // 2), half // 2)

    def rot_copy(src, block, rows, number, l, s):
        return pltpu.make_async_remote_copy(
            src_ref=src,
            dst_ref=rot.at[block, rows, :],
            send_sem=rot_send.at[number],
            recv_sem=rot_recv.at[number],
            device_id=(l, s),
            device_id_type=MESH,
        )

    to_right = rot_copy(rot_hbm.at[half_rows, :], x, half_rows, 0, me, right)
    to_left = rot_copy(rot_hbm.at[half_rows, :], x, half_rows, 1, me, left)
    to_right.start()
    to_left.start()

    for load in loads[:4]:
        load.wait()
    for swap in swaps:
        swap.wait_recv()
    row_iota = lax.broadcasted_iota(jnp.int32, (ROWS_G, 1), 0)
    lane_iota = lax.broadcasted_iota(jnp.int32, (1, LANES), 1)

    def row_copy(g, j, l):
        return pltpu.make_async_remote_copy(
            src_ref=outb.at[g, j],
            dst_ref=inb.at[g, z],
            send_sem=out_sem.at[g],
            recv_sem=in_sem.at[g],
            device_id=(l, x),
            device_id_type=MESH,
        )

    def send_group(g, carry):
        to_y = lax.rem(y + g, NY)
        to_z = lax.rem(z + row_iota // (NC * CAP), NZ)
        wanted = (to_y * NZ + to_z) * (NC * CAP) + lax.rem(row_iota, NC * CAP)
        made = jnp.zeros((ROWS_G, D), F32)
        code_tile = jnp.zeros((ROWS_G, LANES), F32)
        ids = jnp.zeros((ROWS_G, 1), F32)
        for c in range(NC):
            list_id = idx[c]
            owner = list_id // LIST_DEV
            target = (owner // NC * NC + c) * CAP + slot[c]
            match = (wanted == target) & (lax.rem(owner, NC) == core)
            place = jnp.where(match, 1.0, 0.0).astype(BF)
            local = lax.rem(list_id, LIST_DEV).astype(F32) + 4.0
            ids += jnp.sum(jnp.where(match, local, 0.0), axis=1, keepdims=True)
            code_tile += jnp.dot(
                place, (codes[c] + 1).astype(F32).astype(BF), preferred_element_type=F32
            )
            made += jnp.dot(place, emb[c], preferred_element_type=F32)
        id_int = ids.astype(jnp.int32)
        ids_tile = jnp.where(
            lane_iota < LANES // 2, (id_int // 4).astype(F32), lax.rem(id_int, 4).astype(F32)
        )
        outb[g, :, :, 0:D] = made.astype(BF).reshape(CHIPS_G, NC * CAP, D)
        outb[g, :, :, D : D + LANES] = code_tile.astype(BF).reshape(CHIPS_G, NC * CAP, LANES)
        outb[g, :, :, D + LANES : MW] = ids_tile.astype(BF).reshape(CHIPS_G, NC * CAP, LANES)

        def send(j, carry):
            row_copy(g, j, (to_y * NZ + lax.rem(z + j, NZ)) * NC + core).start()
            return carry

        lax.fori_loop(jnp.where(g == 0, 1, 0), CHIPS_G, send, 0)
        return carry

    lax.fori_loop(0, GROUPS, send_group, 0)
    own_block = pltpu.make_async_copy(outb.at[0, 0], inb.at[0, z], own_sem.at[0])
    own_block.start()

    def to_sibling(block, number):
        copy = rot_copy(rot.at[block, half_rows, :], block, half_rows, number, sibling, x)
        copy.start()
        return copy

    to_right.wait_recv()
    on_right = rot_copy(rot.at[left, quarter_a, :], left, quarter_a, 2, me, right)
    on_right.start()
    to_left.wait_recv()
    on_left = rot_copy(rot.at[right, quarter_b, :], right, quarter_b, 3, me, left)
    on_left.start()
    shared = [to_sibling(left, 4), to_sibling(right, 5)]
    on_right.wait_recv()
    on_left.wait_recv()
    shared.append(to_sibling(across, 6))
    for load in loads[4:]:
        load.wait()
    own_block.wait()
    for copy in shared:
        copy.wait_recv()

    list_iota = lax.broadcasted_iota(jnp.int32, (1, LIST_DEV), 1)
    row_of_sums = lax.broadcasted_iota(jnp.int32, (1, OWNERS, 1), 1)
    entry_iota = lax.rem(row_of_sums, CHIPS) * NC + row_of_sums // CHIPS
    sum_row = lax.broadcasted_iota(jnp.int32, (LANES, 1), 0)
    is_count = lax.rem(sum_row, DSUB + 1) == DSUB
    same = lax.broadcasted_iota(jnp.int32, (LANES, LANES), 0) == lax.broadcasted_iota(
        jnp.int32, (LANES, LANES), 1
    )
    unit = jnp.where(same, 1.0, 0.0).astype(BF)

    def group_copy(g, many):
        return pltpu.make_async_remote_copy(
            src_ref=outb.at[g, 0:many],
            dst_ref=inb.at[g, 0:many],
            send_sem=out_sem.at[g],
            recv_sem=in_sem.at[g],
            device_id=(sibling, x),
            device_id_type=MESH,
        )

    def pay_copy(g, dt):
        to = lax.rem(x + dt, NX)
        return pltpu.make_async_remote_copy(
            src_ref=pay_out.at[g, to],
            dst_ref=pay_in.at[g, :, pl.ds(pl.multiple_of(x * ROWS_G, ROWS_G), ROWS_G)],
            send_sem=pay_send.at[g, dt],
            recv_sem=pay_recv.at[g, dt],
            device_id=(me, to),
            device_id_type=MESH,
        )

    def store_copy(g, s):
        from_y = lax.rem(y - g + NY, NY)
        to = pl.multiple_of(s * (OWNERS * CAP) + from_y * ROWS_G, ROWS_G)
        return pltpu.make_async_copy(
            pay_in.at[g, 0:COLS, s * ROWS_G : (s + 1) * ROWS_G],
            store_hbm.at[:, pl.ds(to, ROWS_G)],
            store_sem.at[g, s],
        )

    def rotate_group(g):
        @pl.when(g == 0)
        def _():
            group_copy(0, CHIPS_G - 1).wait_recv()

        @pl.when(g > 0)
        def _():
            group_copy(g, CHIPS_G).wait_recv()

        ids_tile = inb[g, :, :, D + LANES : MW].astype(F32).reshape(ROWS_G, LANES)
        list_row = (
            ids_tile[:, 0:1] * 4.0 + ids_tile[:, LANES // 2 : LANES // 2 + 1] - 4.0
        ).astype(jnp.int32)
        chosen = jnp.where(list_row == list_iota, 1.0, 0.0).astype(BF)
        for part in range(2):
            cut = slice(part * HALF, (part + 1) * HALF)
            picked = jnp.dot(chosen, cent[:, cut], preferred_element_type=F32)
            rows = inb[g, :, :, cut].astype(F32).reshape(ROWS_G, HALF)
            res[:, cut] = (rows - picked).astype(BF)
        code_tile = inb[g, :, :, D : D + LANES].reshape(ROWS_G, LANES)
        code_rows = lax.dot_general(unit, code_tile, NT, preferred_element_type=F32).astype(BF)
        for t in range(NX):
            turned = lax.dot_general(rot[t], res[...], NT, preferred_element_type=F32)
            pay_out[g, t, 0:COLS, :] = turned.astype(BF)
            pay_out[g, t, COLS:PAY, :] = code_rows[t * SUBS_DEV : (t + 1) * SUBS_DEV, :]
        for dt in (2, 1, 3):
            pay_copy(g, dt).start()
        own = pl.ds(pl.multiple_of(x * ROWS_G, ROWS_G), ROWS_G)
        pay_in[g, :, own] = pay_out[g, x]

    def count_group(g):
        for dt in range(1, NX):
            pay_copy(g, dt).wait_recv()
        for s in range(NX):
            store_copy(g, s).start()
        upper = (pay_in[g, COLS:PAY, :].astype(F32).astype(jnp.int32) - 1) >> 2
        for part, (first, many) in enumerate(zip(FIRST, SPLIT)):
            value = jnp.dot(
                spread[part * LANES : (part + 1) * LANES, :], pay_in[g], preferred_element_type=F32
            )
            value = jnp.where(is_count, 1.0, value)
            lower = jnp.dot(
                spread[PW + part * LANES : PW + (part + 1) * LANES, :],
                pay_in[g],
                preferred_element_type=F32,
            )
            lower = (lower.astype(jnp.int32) - 1) & 3
            for lo in range(4):
                vals[lo * LANES : (lo + 1) * LANES, :] = jnp.where(lower == lo, value, 0.0).astype(
                    BF
                )
            ones = jnp.where(upper[first : first + many][:, None, :] == entry_iota, 1.0, 0.0)
            hot[0 : many * OWNERS, :] = ones.astype(BF).reshape(many * OWNERS, NX * ROWS_G)
            acc[part, 0 : many * OWNERS, :] += lax.dot_general(
                hot[0 : many * OWNERS, :], vals[...], NT, preferred_element_type=F32
            )

    acc[...] = jnp.zeros_like(acc)

    def both(g, carry):
        @pl.when(g < GROUPS)
        def _():
            rotate_group(g)

        @pl.when(g > 0)
        def _():
            count_group(g - 1)

        return carry

    lax.fori_loop(0, GROUPS + 1, both, 0)

    subspace = lane_iota // (DSUB + 1)
    for part, many in enumerate(SPLIT):
        for lo in range(4):
            cut = slice(lo * LANES, (lo + 1) * LANES)
            total = jnp.zeros((OWNERS, LANES), F32)
            for i in range(many):
                total = jnp.where(
                    subspace == i, acc[part, i * OWNERS : (i + 1) * OWNERS, cut], total
                )
            sum_out[:, :, part * 4 + lo, :] = total.reshape(NC, CHIPS, LANES)

    pair = pltpu.make_async_remote_copy(
        src_ref=sum_out.at[1 - core],
        dst_ref=sum_pair,
        send_sem=pair_send,
        recv_sem=pair_recv,
        device_id=(sibling, x),
        device_id_type=MESH,
    )
    pair.start()
    pair.wait_recv()
    sum_mid[...] = sum_out[core] + sum_pair[...]

    def send_sum(k, carry):
        pltpu.make_async_remote_copy(
            src_ref=sum_mid.at[lax.rem(chip + k, CHIPS)],
            dst_ref=sum_in.at[k],
            send_sem=sum_send,
            recv_sem=sum_recv,
            device_id=(peer_of(k), x),
            device_id_type=MESH,
        ).start()
        return carry

    lax.fori_loop(1, CHIPS, send_sum, 0)
    sum_in[0] = sum_mid[chip]
    all_sums = pltpu.make_async_remote_copy(
        src_ref=sum_mid.at[1:CHIPS],
        dst_ref=sum_in.at[1:CHIPS],
        send_sem=sum_send,
        recv_sem=sum_recv,
        device_id=(sibling, x),
        device_id_type=MESH,
    )
    all_sums.wait_recv()
    total = jnp.sum(sum_in[...], axis=0)
    sums = jnp.zeros((4, COLS), F32)
    counts = jnp.zeros((4, COLS), F32)
    for part in range(len(SPLIT)):
        tile = total[part * 4 : part * 4 + 4, :]
        sums += jnp.dot(
            tile, back[0, part], preferred_element_type=F32, precision=lax.Precision.HIGHEST
        )
        counts += jnp.dot(
            tile, back[1, part], preferred_element_type=F32, precision=lax.Precision.HIGHEST
        )
    book_ref[...] = (sums + ANCHOR * old[...]) / (counts + ANCHOR)

    for swap in swaps:
        swap.wait_send()
    group_copy(0, CHIPS_G - 1).wait_send()
    for g in range(1, GROUPS):
        group_copy(g, CHIPS_G).wait_send()
    for copy in [to_right, to_left, on_right, on_left] + shared:
        copy.wait_send()
    for g in range(GROUPS):
        for dt in range(1, NX):
            pay_copy(g, dt).wait_send()
    pair.wait_send()
    all_sums.wait_send()
    for g in range(GROUPS):
        for s in range(NX):
            store_copy(g, s).wait()


def shards(embeddings, coarse_list_index, slots, codes, centroids, rotation, old_codebook):
    spread, back = layout_tables()
    vmem = pl.BlockSpec(memory_space=pltpu.VMEM)
    anywhere = pl.BlockSpec(memory_space=pl.ANY)
    dma = pltpu.SemaphoreType.DMA
    store, book = pl.pallas_call(
        kernel,
        out_shape=(
            jax.ShapeDtypeStruct((COLS, OWNERS * NX * CAP), BF),
            jax.ShapeDtypeStruct((CENT // OWNERS, COLS), F32),
        ),
        in_specs=[anywhere] * 9,
        out_specs=(anywhere, vmem),
        scratch_shapes=[
            pltpu.VMEM((NC, ROW_DEV, D), BF),
            pltpu.VMEM((NC, 1, ROW_DEV), jnp.int32),
            pltpu.VMEM((NC, 1, ROW_DEV), jnp.int32),
            pltpu.VMEM((NC, ROW_DEV, LANES), jnp.int32),
            pltpu.VMEM((LIST_DEV, D), BF),
            pltpu.VMEM((NX, COLS, D), BF),
            pltpu.VMEM((CENT // OWNERS, COLS), F32),
            pltpu.VMEM((2 * PW, PAY), BF),
            pltpu.VMEM((2, len(SPLIT), LANES, COLS), F32),
            pltpu.VMEM((GROUPS, CHIPS_G, NC * CAP, MW), BF),
            pltpu.VMEM((GROUPS, CHIPS_G, NC * CAP, MW), BF),
            pltpu.VMEM((ROWS_G, D), BF),
            pltpu.VMEM((GROUPS, NX, PAY, ROWS_G), BF),
            pltpu.VMEM((GROUPS, PAY, NX * ROWS_G), BF),
            pltpu.VMEM((SPLIT[0] * OWNERS, NX * ROWS_G), BF),
            pltpu.VMEM((4 * LANES, NX * ROWS_G), BF),
            pltpu.VMEM((len(SPLIT), SPLIT[0] * OWNERS, 4 * LANES), F32),
            pltpu.VMEM((NC, CHIPS, 12, LANES), F32),
            pltpu.VMEM((CHIPS, 12, LANES), F32),
            pltpu.VMEM((CHIPS, 12, LANES), F32),
            pltpu.VMEM((CHIPS, 12, LANES), F32),
            dma((9,)),
            dma((4,)),
            dma((4,)),
            dma((GROUPS,)),
            dma((GROUPS,)),
            dma((7,)),
            dma((7,)),
            dma((GROUPS, NX)),
            dma((GROUPS, NX)),
            dma((1,)),
            dma(()),
            dma(()),
            dma(()),
            dma(()),
            dma((GROUPS, NX)),
        ],
        compiler_params=pltpu.CompilerParams(
            collective_id=0, has_side_effects=True, vmem_limit_bytes=56 * 2**20
        ),
    )(
        embeddings,
        coarse_list_index.reshape(1, ROW_DEV),
        slots.reshape(1, ROW_DEV),
        codes,
        centroids,
        rotation.T,
        old_codebook,
        jnp.asarray(spread, BF),
        jnp.asarray(back, F32),
    )
    return store.T, book


def solution(mesh):
    return jax.shard_map(
        shards,
        mesh=mesh,
        in_specs=(
            P(("list", "sub"), None),
            P(("list", "sub")),
            P(("list", "sub")),
            P(("list", "sub"), None),
            P("list", None),
            P(None, "sub"),
            P("list", "sub"),
        ),
        out_specs=(P("list", "sub"), P("list", "sub")),
        check_vma=False,
    )
```

```python
import functools

import jax
import jax.numpy as jnp
import numpy as np
from jax import lax
from jax.experimental import pallas as pl
from jax.experimental.pallas import tpu as pltpu
from jax.sharding import PartitionSpec as P

MESH = pl.DeviceIdType.MESH
NY, NZ, NC, NX = 4, 8, 2, 4
OWNERS = NY * NZ * NC
ROW_DEV = 256
CAP = 8
D = 1280
HALF = D // 2
COLS = D // NX
CENT = 256
LIST_DEV = 1024
SUBS_DEV = 32
DSUB = 10
GROUPS = 4
CHIPS_G = 8
CHIPS = NY * NZ
ROWS_G = CHIPS_G * NC * CAP
MW = D + 128
PW = 384
PAY = COLS + SUBS_DEV
NT = (((1,), (1,)), ((), ()))
LANES = 128
SPLIT = (11, 11, 10)
FIRST = (0, 11, 22)
ANCHOR = 64.0
BF = jnp.bfloat16
F32 = jnp.float32


def layout_tables():
    spread = np.zeros((2 * PW, PAY), np.float32)
    back = np.zeros((2, len(SPLIT), LANES, COLS), np.float32)
    for g, (first, many) in enumerate(zip(FIRST, SPLIT)):
        for i in range(many):
            m = first + i
            for d in range(DSUB + 1):
                lane = i * (DSUB + 1) + d
                spread[PW + g * LANES + lane, COLS + m] = 1
                if d < DSUB:
                    spread[g * LANES + lane, m * DSUB + d] = 1
                    back[0, g, lane, m * DSUB + d] = 1
                    back[1, g, i * (DSUB + 1) + DSUB, m * DSUB + d] = 1
    return spread, back


def kernel(
    emb_hbm,
    idx_hbm,
    slot_hbm,
    codes_hbm,
    cent_hbm,
    rot_hbm,
    old_hbm,
    spread_hbm,
    back_hbm,
    store_hbm,
    book_ref,
    emb,
    idx,
    slot,
    codes,
    cent,
    rot,
    old,
    spread,
    back,
    outb,
    inb,
    ids_out,
    ids_in,
    res,
    code_rows,
    pay_out,
    pay_in,
    hot,
    vals,
    acc,
    sum_out,
    sum_pair,
    sum_mid,
    sum_in,
    load_sem,
    swap_send,
    swap_recv,
    out_sem,
    in_sem,
    ids_send,
    ids_recv,
    rot_send,
    rot_recv,
    pay_send,
    pay_recv,
    own_sem,
    pair_send,
    pair_recv,
    sum_send,
    sum_recv,
    store_sem,
):
    me = lax.axis_index("list")
    x = lax.axis_index("sub")
    core = lax.rem(me, NC)
    chip = me // NC
    z = lax.rem(chip, NZ)
    y = chip // NZ
    sibling = me + 1 - 2 * core
    right, left = lax.rem(x + 1, NX), lax.rem(x + NX - 1, NX)
    across = lax.rem(x + 2, NX)

    own_rows = pl.ds(pl.multiple_of(core * ROW_DEV, ROW_DEV), ROW_DEV)
    sources = [
        (emb_hbm, emb.at[own_rows, 0:D]),
        (idx_hbm, idx.at[core]),
        (slot_hbm, slot.at[core]),
        (codes_hbm, codes.at[own_rows, :]),
    ]
    loads = [
        pltpu.make_async_copy(src, dst, load_sem.at[i]) for i, (src, dst) in enumerate(sources)
    ]
    later = [(cent_hbm, cent), (rot_hbm, rot.at[x]), (spread_hbm, spread), (back_hbm, back)]
    later.append((old_hbm, old))
    loads += [
        pltpu.make_async_copy(src, dst, load_sem.at[4 + i]) for i, (src, dst) in enumerate(later)
    ]
    for load in loads:
        load.start()

    barrier = pltpu.get_barrier_semaphore()

    def peer_of(k):
        return lax.rem(chip + k, CHIPS) * NC + core

    def greet(k, carry):
        pl.semaphore_signal(barrier, inc=1, device_id=(peer_of(k), x), device_id_type=MESH)
        return carry

    lax.fori_loop(1, CHIPS, greet, 0)
    pl.semaphore_signal(barrier, inc=1, device_id=(sibling, x), device_id_type=MESH)
    for k in range(1, NX):
        pl.semaphore_signal(
            barrier, inc=1, device_id=(me, lax.rem(x + k, NX)), device_id_type=MESH
        )
    pl.semaphore_wait(barrier, CHIPS + NX - 1)

    swaps = [
        pltpu.make_async_remote_copy(
            src_ref=src,
            dst_ref=dst,
            send_sem=swap_send.at[i],
            recv_sem=swap_recv.at[i],
            device_id=(sibling, x),
            device_id_type=MESH,
        )
        for i, (src, dst) in enumerate(sources)
    ]
    for swap in swaps:
        swap.start()

    half = COLS // 2
    half_rows = pl.ds(pl.multiple_of(core * half, half), half)
    quarter_a = pl.ds(pl.multiple_of(core * half, half // 2), half // 2)
    quarter_b = pl.ds(pl.multiple_of(core * half + half // 2, half // 2), half // 2)

    def rot_copy(src, block, rows, number, l, s):
        return pltpu.make_async_remote_copy(
            src_ref=src,
            dst_ref=rot.at[block, rows, :],
            send_sem=rot_send.at[number],
            recv_sem=rot_recv.at[number],
            device_id=(l, s),
            device_id_type=MESH,
        )

    to_right = rot_copy(rot_hbm.at[half_rows, :], x, half_rows, 0, me, right)
    to_left = rot_copy(rot_hbm.at[half_rows, :], x, half_rows, 1, me, left)
    to_right.start()
    to_left.start()

    for load in loads[:4]:
        load.wait()
    for swap in swaps:
        swap.wait_recv()
    emb[:, D:MW] = (codes[...] + 1).astype(F32).astype(BF)
    keys, uppers, lowers = [], [], []
    for c in range(NC):
        list_id = idx[c]
        owner = list_id // LIST_DEV
        key = (owner // NC * NC + c) * CAP + slot[c]
        keys.append(jnp.where(lax.rem(owner, NC) == core, key, -1))
        local = lax.rem(list_id, LIST_DEV)
        uppers.append((local // 4 + 1).astype(F32).astype(BF))
        lowers.append(lax.rem(local, 4).astype(F32).astype(BF))
    key = jnp.concatenate(keys, axis=1)
    upper_id = jnp.concatenate(uppers, axis=1)
    lower_id = jnp.concatenate(lowers, axis=1)
    row_iota = lax.broadcasted_iota(jnp.int32, (ROWS_G, 1), 0)
    lane_iota = lax.broadcasted_iota(jnp.int32, (1, LANES), 1)

    def row_copy(g, l, to_z):
        return pltpu.make_async_remote_copy(
            src_ref=outb.at[g, to_z],
            dst_ref=inb.at[g, z],
            send_sem=out_sem.at[g],
            recv_sem=in_sem.at[g],
            device_id=(l, x),
            device_id_type=MESH,
        )

    def ids_copy(g, l):
        return pltpu.make_async_remote_copy(
            src_ref=ids_out.at[g],
            dst_ref=ids_in.at[g, z],
            send_sem=ids_send.at[g],
            recv_sem=ids_recv.at[g],
            device_id=(l, x),
            device_id_type=MESH,
        )

    def send_group(g, carry):
        to_y = lax.rem(y + g, NY)
        place = jnp.where(to_y * ROWS_G + row_iota == key, 1.0, 0.0).astype(BF)
        ids = 4.0 * lax.dot_general(
            upper_id, place, NT, preferred_element_type=F32
        ) + lax.dot_general(lower_id, place, NT, preferred_element_type=F32)
        ids_out[g] = ids.astype(jnp.int32)
        made = jnp.dot(place, emb[...], preferred_element_type=F32)
        outb[g] = made.astype(BF).reshape(CHIPS_G, NC * CAP, MW)

        def send(k, carry):
            step = jnp.where(lax.rem(k, 2) == 1, (k + 1) // 2, NZ - k // 2)
            to_z = lax.rem(z + step, NZ)
            l = (to_y * NZ + to_z) * NC + core
            ids_copy(g, l).start()
            row_copy(g, l, to_z).start()
            return carry

        lax.fori_loop(jnp.where(g == 0, 1, 0), CHIPS_G, send, 0)
        return carry

    send_group(0, 0)
    own_block = pltpu.make_async_copy(outb.at[0, z], inb.at[0, z], own_sem.at[0])
    own_block.start()
    ids_in[0, z] = ids_out[0]
    lax.fori_loop(1, GROUPS, send_group, 0)

    def to_sibling(block, number):
        copy = rot_copy(rot.at[block, half_rows, :], block, half_rows, number, sibling, x)
        copy.start()
        return copy

    to_right.wait_recv()
    on_right = rot_copy(rot.at[left, quarter_a, :], left, quarter_a, 2, me, right)
    on_right.start()
    to_left.wait_recv()
    on_left = rot_copy(rot.at[right, quarter_b, :], right, quarter_b, 3, me, left)
    on_left.start()
    shared = [to_sibling(left, 4), to_sibling(right, 5)]
    on_right.wait_recv()
    on_left.wait_recv()
    shared.append(to_sibling(across, 6))
    for load in loads[4:]:
        load.wait()
    own_block.wait()
    for copy in shared:
        copy.wait_recv()

    list_iota = lax.broadcasted_iota(jnp.int32, (1, LIST_DEV), 1)
    row_of_sums = lax.broadcasted_iota(jnp.int32, (1, OWNERS, 1), 1)
    entry_iota = lax.rem(row_of_sums, CHIPS) * NC + row_of_sums // CHIPS
    sum_row = lax.broadcasted_iota(jnp.int32, (LANES, 1), 0)
    is_count = lax.rem(sum_row, DSUB + 1) == DSUB
    same = lax.broadcasted_iota(jnp.int32, (LANES, LANES), 0) == lax.broadcasted_iota(
        jnp.int32, (LANES, LANES), 1
    )
    lane_of_row = lax.broadcasted_iota(
        jnp.int32, (CHIPS_G, NC * CAP, LANES), 2
    ) == z * NC * CAP + lax.broadcasted_iota(jnp.int32, (CHIPS_G, NC * CAP, LANES), 1)
    unit = jnp.where(same, 1.0, 0.0).astype(BF)

    def group_copy(g, many):
        return pltpu.make_async_remote_copy(
            src_ref=outb.at[g, 0:many],
            dst_ref=inb.at[g, 0:many],
            send_sem=out_sem.at[g],
            recv_sem=in_sem.at[g],
            device_id=(sibling, x),
            device_id_type=MESH,
        )

    def ids_group_copy(g, many):
        return pltpu.make_async_remote_copy(
            src_ref=ids_in.at[g, 0:many],
            dst_ref=ids_in.at[g, 0:many],
            send_sem=ids_send.at[g],
            recv_sem=ids_recv.at[g],
            device_id=(sibling, x),
            device_id_type=MESH,
        )

    def pay_copy(g, dt):
        to = lax.rem(x + dt, NX)
        return pltpu.make_async_remote_copy(
            src_ref=pay_out.at[g, to],
            dst_ref=pay_in.at[g, :, pl.ds(pl.multiple_of(x * ROWS_G, ROWS_G), ROWS_G)],
            send_sem=pay_send.at[g, dt],
            recv_sem=pay_recv.at[g, dt],
            device_id=(me, to),
            device_id_type=MESH,
        )

    def store_copy(g, s):
        from_y = lax.rem(y - g + NY, NY)
        to = pl.multiple_of(s * (OWNERS * CAP) + from_y * ROWS_G, ROWS_G)
        return pltpu.make_async_copy(
            pay_in.at[g, 0:COLS, s * ROWS_G : (s + 1) * ROWS_G],
            store_hbm.at[:, pl.ds(to, ROWS_G)],
            store_sem.at[g, s],
        )

    def rotate_group(g):
        @pl.when(g == 0)
        def _():
            group_copy(0, CHIPS_G - 1).wait_recv()
            ids_group_copy(0, CHIPS_G - 1).wait_recv()

        @pl.when(g > 0)
        def _():
            group_copy(g, CHIPS_G).wait_recv()
            ids_group_copy(g, CHIPS_G).wait_recv()

        ids = jnp.where(lane_of_row, ids_in[g].astype(F32), 0.0)
        list_row = jnp.sum(ids, axis=2, keepdims=True).reshape(ROWS_G, 1).astype(jnp.int32) - 4
        chosen = jnp.where(list_row == list_iota, 1.0, 0.0).astype(BF)
        for part in range(2):
            cut = slice(part * HALF, (part + 1) * HALF)
            picked = jnp.dot(chosen, cent[:, cut], preferred_element_type=F32)
            rows = inb[g, :, :, cut].astype(F32).reshape(ROWS_G, HALF)
            res[:, cut] = (rows - picked).astype(BF)
        code_tile = inb[g, :, :, D:MW].reshape(ROWS_G, LANES)
        code_rows[...] = lax.dot_general(unit, code_tile, NT, preferred_element_type=F32).astype(BF)
        own = pl.ds(pl.multiple_of(x * ROWS_G, ROWS_G), ROWS_G)
        for dt in (2, 1, 3, 0):
            t = lax.rem(x + dt, NX)
            turned = lax.dot_general(rot[t], res[...], NT, preferred_element_type=F32).astype(BF)
            mine = code_rows[pl.ds(pl.multiple_of(t * SUBS_DEV, SUBS_DEV), SUBS_DEV), :]
            if dt:
                pay_out[g, t, 0:COLS, :] = turned
                pay_out[g, t, COLS:PAY, :] = mine
                pay_copy(g, dt).start()
            else:
                pay_in[g, 0:COLS, own] = turned
                pay_in[g, COLS:PAY, own] = mine

    def count_group(g):
        for dt in range(1, NX):
            pay_copy(g, dt).wait_recv()
        for s in range(NX):
            store_copy(g, s).start()
        upper = (pay_in[g, COLS:PAY, :].astype(F32).astype(jnp.int32) - 1) >> 2
        for part, (first, many) in enumerate(zip(FIRST, SPLIT)):
            value = jnp.dot(
                spread[part * LANES : (part + 1) * LANES, :], pay_in[g], preferred_element_type=F32
            )
            value = jnp.where(is_count, 1.0, value)
            lower = jnp.dot(
                spread[PW + part * LANES : PW + (part + 1) * LANES, :],
                pay_in[g],
                preferred_element_type=F32,
            )
            lower = (lower.astype(jnp.int32) - 1) & 3
            for lo in range(4):
                vals[lo * LANES : (lo + 1) * LANES, :] = jnp.where(lower == lo, value, 0.0).astype(
                    BF
                )
            ones = jnp.where(upper[first : first + many][:, None, :] == entry_iota, 1.0, 0.0)
            hot[0 : many * OWNERS, :] = ones.astype(BF).reshape(many * OWNERS, NX * ROWS_G)
            acc[part, 0 : many * OWNERS, :] += lax.dot_general(
                hot[0 : many * OWNERS, :], vals[...], NT, preferred_element_type=F32
            )

    acc[...] = jnp.zeros_like(acc)

    def both(g, carry):
        @pl.when(g < GROUPS)
        def _():
            rotate_group(g)

        @pl.when(g > 0)
        def _():
            count_group(g - 1)

        return carry

    lax.fori_loop(0, GROUPS + 1, both, 0)

    subspace = lane_iota // (DSUB + 1)
    for part, many in enumerate(SPLIT):
        for lo in range(4):
            cut = slice(lo * LANES, (lo + 1) * LANES)
            total = jnp.zeros((OWNERS, LANES), F32)
            for i in range(many):
                total = jnp.where(
                    subspace == i, acc[part, i * OWNERS : (i + 1) * OWNERS, cut], total
                )
            sum_out[:, :, part * 4 + lo, :] = total.reshape(NC, CHIPS, LANES)

    pair = pltpu.make_async_remote_copy(
        src_ref=sum_out.at[1 - core],
        dst_ref=sum_pair,
        send_sem=pair_send,
        recv_sem=pair_recv,
        device_id=(sibling, x),
        device_id_type=MESH,
    )
    pair.start()
    pair.wait_recv()
    sum_mid[...] = sum_out[core] + sum_pair[...]

    def send_sum(k, carry):
        pltpu.make_async_remote_copy(
            src_ref=sum_mid.at[lax.rem(chip + k, CHIPS)],
            dst_ref=sum_in.at[k],
            send_sem=sum_send,
            recv_sem=sum_recv,
            device_id=(peer_of(k), x),
            device_id_type=MESH,
        ).start()
        return carry

    lax.fori_loop(1, CHIPS, send_sum, 0)
    sum_in[0] = sum_mid[chip]
    all_sums = pltpu.make_async_remote_copy(
        src_ref=sum_mid.at[1:CHIPS],
        dst_ref=sum_in.at[1:CHIPS],
        send_sem=sum_send,
        recv_sem=sum_recv,
        device_id=(sibling, x),
        device_id_type=MESH,
    )
    all_sums.wait_recv()
    total = jnp.sum(sum_in[...], axis=0)
    sums = jnp.zeros((4, COLS), F32)
    counts = jnp.zeros((4, COLS), F32)
    for part in range(len(SPLIT)):
        tile = total[part * 4 : part * 4 + 4, :]
        sums += jnp.dot(
            tile, back[0, part], preferred_element_type=F32, precision=lax.Precision.HIGHEST
        )
        counts += jnp.dot(
            tile, back[1, part], preferred_element_type=F32, precision=lax.Precision.HIGHEST
        )
    book_ref[...] = (sums + ANCHOR * old[...]) / (counts + ANCHOR)

    for swap in swaps:
        swap.wait_send()
    group_copy(0, CHIPS_G - 1).wait_send()
    ids_group_copy(0, CHIPS_G - 1).wait_send()
    for g in range(1, GROUPS):
        group_copy(g, CHIPS_G).wait_send()
        ids_group_copy(g, CHIPS_G).wait_send()
    for copy in [to_right, to_left, on_right, on_left] + shared:
        copy.wait_send()
    for g in range(GROUPS):
        for dt in range(1, NX):
            pay_copy(g, dt).wait_send()
    pair.wait_send()
    all_sums.wait_send()
    for g in range(GROUPS):
        for s in range(NX):
            store_copy(g, s).wait()


def shards(embeddings, coarse_list_index, slots, codes, centroids, rotation, old_codebook):
    spread, back = layout_tables()
    vmem = pl.BlockSpec(memory_space=pltpu.VMEM)
    anywhere = pl.BlockSpec(memory_space=pl.ANY)
    dma = pltpu.SemaphoreType.DMA
    store, book = pl.pallas_call(
        kernel,
        out_shape=(
            jax.ShapeDtypeStruct((COLS, OWNERS * NX * CAP), BF),
            jax.ShapeDtypeStruct((CENT // OWNERS, COLS), F32),
        ),
        in_specs=[anywhere] * 9,
        out_specs=(anywhere, vmem),
        scratch_shapes=[
            pltpu.VMEM((NC * ROW_DEV, MW), BF),
            pltpu.VMEM((NC, 1, ROW_DEV), jnp.int32),
            pltpu.VMEM((NC, 1, ROW_DEV), jnp.int32),
            pltpu.VMEM((NC * ROW_DEV, LANES), jnp.int32),
            pltpu.VMEM((LIST_DEV, D), BF),
            pltpu.VMEM((NX, COLS, D), BF),
            pltpu.VMEM((CENT // OWNERS, COLS), F32),
            pltpu.VMEM((2 * PW, PAY), BF),
            pltpu.VMEM((2, len(SPLIT), LANES, COLS), F32),
            pltpu.VMEM((GROUPS, CHIPS_G, NC * CAP, MW), BF),
            pltpu.VMEM((GROUPS, CHIPS_G, NC * CAP, MW), BF),
            pltpu.VMEM((GROUPS, 1, LANES), jnp.int32),
            pltpu.VMEM((GROUPS, CHIPS_G, 1, LANES), jnp.int32),
            pltpu.VMEM((ROWS_G, D), BF),
            pltpu.VMEM((LANES, ROWS_G), BF),
            pltpu.VMEM((GROUPS, NX, PAY, ROWS_G), BF),
            pltpu.VMEM((GROUPS, PAY, NX * ROWS_G), BF),
            pltpu.VMEM((SPLIT[0] * OWNERS, NX * ROWS_G), BF),
            pltpu.VMEM((4 * LANES, NX * ROWS_G), BF),
            pltpu.VMEM((len(SPLIT), SPLIT[0] * OWNERS, 4 * LANES), F32),
            pltpu.VMEM((NC, CHIPS, 12, LANES), F32),
            pltpu.VMEM((CHIPS, 12, LANES), F32),
            pltpu.VMEM((CHIPS, 12, LANES), F32),
            pltpu.VMEM((CHIPS, 12, LANES), F32),
            dma((9,)),
            dma((4,)),
            dma((4,)),
            dma((GROUPS,)),
            dma((GROUPS,)),
            dma((GROUPS,)),
            dma((GROUPS,)),
            dma((7,)),
            dma((7,)),
            dma((GROUPS, NX)),
            dma((GROUPS, NX)),
            dma((1,)),
            dma(()),
            dma(()),
            dma(()),
            dma(()),
            dma((GROUPS, NX)),
        ],
        compiler_params=pltpu.CompilerParams(
            collective_id=0, has_side_effects=True, vmem_limit_bytes=56 * 2**20
        ),
    )(
        embeddings,
        coarse_list_index.reshape(1, ROW_DEV),
        slots.reshape(1, ROW_DEV),
        codes,
        centroids,
        rotation.T,
        old_codebook,
        jnp.asarray(spread, BF),
        jnp.asarray(back, F32),
    )
    return store.T, book


def solution(mesh):
    return jax.shard_map(
        shards,
        mesh=mesh,
        in_specs=(
            P(("list", "sub"), None),
            P(("list", "sub")),
            P(("list", "sub")),
            P(("list", "sub"), None),
            P("list", None),
            P(None, "sub"),
            P("list", "sub"),
        ),
        out_specs=(P("list", "sub"), P("list", "sub")),
        check_vma=False,
    )
```

```python
import functools

import jax
import jax.numpy as jnp
import numpy as np
from jax import lax
from jax.experimental import pallas as pl
from jax.experimental.pallas import tpu as pltpu
from jax.sharding import PartitionSpec as P

MESH = pl.DeviceIdType.MESH
NY, NZ, NC, NX = 4, 8, 2, 4
OWNERS = NY * NZ * NC
ROW_DEV = 256
CAP = 8
D = 1280
HALF = D // 2
COLS = D // NX
CENT = 256
LIST_DEV = 1024
SUBS_DEV = 32
DSUB = 10
GROUPS = 4
CHIPS_G = 8
CHIPS = NY * NZ
ROWS_G = CHIPS_G * NC * CAP
MW = D + 128
PW = 384
PAY = COLS + SUBS_DEV
NT = (((1,), (1,)), ((), ()))
LANES = 128
SPLIT = (11, 11, 10)
FIRST = (0, 11, 22)
ANCHOR = 64.0
BF = jnp.bfloat16
F32 = jnp.float32


def layout_tables():
    spread = np.zeros((2 * PW, PAY), np.float32)
    back = np.zeros((PW, 2 * PW), np.float32)
    for g, (first, many) in enumerate(zip(FIRST, SPLIT)):
        for i in range(many):
            m = first + i
            for d in range(DSUB + 1):
                lane = i * (DSUB + 1) + d
                spread[PW + g * LANES + lane, COLS + m] = 1
                if d < DSUB:
                    spread[g * LANES + lane, m * DSUB + d] = 1
                    back[g * LANES + lane, m * DSUB + d] = 1
                    back[g * LANES + i * (DSUB + 1) + DSUB, PW + m * DSUB + d] = 1
    return spread, back


def kernel(
    emb_hbm,
    idx_hbm,
    slot_hbm,
    codes_hbm,
    cent_hbm,
    rot_hbm,
    old_hbm,
    spread_hbm,
    back_hbm,
    store_hbm,
    book_ref,
    emb,
    idx,
    slot,
    codes,
    cent,
    rot,
    old,
    spread,
    back,
    outb,
    inb,
    ids_out,
    ids_in,
    res,
    code_rows,
    pay_out,
    pay_in,
    hot,
    vals,
    acc,
    sum_out,
    sum_pair,
    sum_mid,
    sum_in,
    load_sem,
    swap_send,
    swap_recv,
    out_sem,
    in_sem,
    ids_send,
    ids_recv,
    rot_send,
    rot_recv,
    pay_send,
    pay_recv,
    own_sem,
    pair_send,
    pair_recv,
    sum_send,
    sum_recv,
    store_sem,
):
    me = lax.axis_index("list")
    x = lax.axis_index("sub")
    core = lax.rem(me, NC)
    chip = me // NC
    z = lax.rem(chip, NZ)
    y = chip // NZ
    sibling = me + 1 - 2 * core
    right, left = lax.rem(x + 1, NX), lax.rem(x + NX - 1, NX)
    across = lax.rem(x + 2, NX)

    own_rows = pl.ds(pl.multiple_of(core * ROW_DEV, ROW_DEV), ROW_DEV)
    sources = [
        (emb_hbm, emb.at[own_rows, 0:D]),
        (idx_hbm, idx.at[core]),
        (slot_hbm, slot.at[core]),
        (codes_hbm, codes.at[own_rows, :]),
    ]
    loads = [
        pltpu.make_async_copy(src, dst, load_sem.at[i]) for i, (src, dst) in enumerate(sources)
    ]
    later = [(cent_hbm, cent), (rot_hbm, rot.at[x]), (spread_hbm, spread), (back_hbm, back)]
    later.append((old_hbm, old))
    loads += [
        pltpu.make_async_copy(src, dst, load_sem.at[4 + i]) for i, (src, dst) in enumerate(later)
    ]
    for load in loads[:4]:
        load.start()

    barrier = pltpu.get_barrier_semaphore()

    def peer_of(k):
        return lax.rem(chip + k, CHIPS) * NC + core

    def greet(k, carry):
        pl.semaphore_signal(barrier, inc=1, device_id=(peer_of(k), x), device_id_type=MESH)
        return carry

    lax.fori_loop(1, CHIPS, greet, 0)
    pl.semaphore_signal(barrier, inc=1, device_id=(sibling, x), device_id_type=MESH)
    for k in range(1, NX):
        pl.semaphore_signal(
            barrier, inc=1, device_id=(me, lax.rem(x + k, NX)), device_id_type=MESH
        )
    pl.semaphore_wait(barrier, CHIPS + NX - 1)

    swaps = [
        pltpu.make_async_remote_copy(
            src_ref=src,
            dst_ref=dst,
            send_sem=swap_send.at[i],
            recv_sem=swap_recv.at[i],
            device_id=(sibling, x),
            device_id_type=MESH,
        )
        for i, (src, dst) in enumerate(sources)
    ]
    for swap in swaps:
        swap.start()

    half = COLS // 2
    half_rows = pl.ds(pl.multiple_of(core * half, half), half)
    quarter_a = pl.ds(pl.multiple_of(core * half, half // 2), half // 2)
    quarter_b = pl.ds(pl.multiple_of(core * half + half // 2, half // 2), half // 2)

    def rot_copy(src, block, rows, number, l, s):
        return pltpu.make_async_remote_copy(
            src_ref=src,
            dst_ref=rot.at[block, rows, :],
            send_sem=rot_send.at[number],
            recv_sem=rot_recv.at[number],
            device_id=(l, s),
            device_id_type=MESH,
        )

    to_right = rot_copy(rot_hbm.at[half_rows, :], x, half_rows, 0, me, right)
    to_left = rot_copy(rot_hbm.at[half_rows, :], x, half_rows, 1, me, left)
    to_right.start()
    to_left.start()
    for load in loads[4:]:
        load.start()

    for load in loads[:4]:
        load.wait()
    for swap in swaps:
        swap.wait_recv()
    emb[:, D:MW] = (codes[...] + 1).astype(F32).astype(BF)
    keys, uppers, lowers = [], [], []
    for c in range(NC):
        list_id = idx[c]
        owner = list_id // LIST_DEV
        key = (owner // NC * NC + c) * CAP + slot[c]
        keys.append(jnp.where(lax.rem(owner, NC) == core, key, -1))
        local = lax.rem(list_id, LIST_DEV)
        uppers.append((local // 4 + 1).astype(F32).astype(BF))
        lowers.append(lax.rem(local, 4).astype(F32).astype(BF))
    key = jnp.concatenate(keys, axis=1)
    upper_id = jnp.concatenate(uppers, axis=1)
    lower_id = jnp.concatenate(lowers, axis=1)
    row_iota = lax.broadcasted_iota(jnp.int32, (ROWS_G, 1), 0)
    lane_iota = lax.broadcasted_iota(jnp.int32, (1, LANES), 1)

    def row_copy(g, l, to_z):
        return pltpu.make_async_remote_copy(
            src_ref=outb.at[g, to_z],
            dst_ref=inb.at[g, z],
            send_sem=out_sem.at[g],
            recv_sem=in_sem.at[g],
            device_id=(l, x),
            device_id_type=MESH,
        )

    def ids_copy(g, l):
        return pltpu.make_async_remote_copy(
            src_ref=ids_out.at[g],
            dst_ref=ids_in.at[g, z],
            send_sem=ids_send.at[g],
            recv_sem=ids_recv.at[g],
            device_id=(l, x),
            device_id_type=MESH,
        )

    def send_group(g, carry):
        to_y = lax.rem(y + g, NY)
        place = jnp.where(to_y * ROWS_G + row_iota == key, 1.0, 0.0).astype(BF)
        ids = 4.0 * lax.dot_general(
            upper_id, place, NT, preferred_element_type=F32
        ) + lax.dot_general(lower_id, place, NT, preferred_element_type=F32)
        ids_out[g] = ids.astype(jnp.int32)
        made = jnp.dot(place, emb[...], preferred_element_type=F32)
        outb[g] = made.astype(BF).reshape(CHIPS_G, NC * CAP, MW)

        def send(k, carry):
            step = NZ // 2 + jnp.where(lax.rem(k, 2) == 1, -((k + 1) // 2), k // 2)
            to_z = lax.rem(z + step, NZ)
            l = (to_y * NZ + to_z) * NC + core
            ids_copy(g, l).start()
            row_copy(g, l, to_z).start()
            return carry

        lax.fori_loop(0, jnp.where(g == 0, CHIPS_G - 1, CHIPS_G), send, 0)
        return carry

    send_group(0, 0)
    own_block = pltpu.make_async_copy(outb.at[0, z], inb.at[0, z], own_sem.at[0])
    own_block.start()
    ids_in[0, z] = ids_out[0]
    lax.fori_loop(1, GROUPS, send_group, 0)

    def to_sibling(block, number):
        copy = rot_copy(rot.at[block, half_rows, :], block, half_rows, number, sibling, x)
        copy.start()
        return copy

    to_right.wait_recv()
    on_right = rot_copy(rot.at[left, quarter_a, :], left, quarter_a, 2, me, right)
    on_right.start()
    to_left.wait_recv()
    on_left = rot_copy(rot.at[right, quarter_b, :], right, quarter_b, 3, me, left)
    on_left.start()
    shared = [to_sibling(left, 4), to_sibling(right, 5)]
    on_right.wait_recv()
    on_left.wait_recv()
    shared.append(to_sibling(across, 6))
    for load in loads[4:]:
        load.wait()
    own_block.wait()
    for copy in shared:
        copy.wait_recv()

    list_iota = lax.broadcasted_iota(jnp.int32, (1, LIST_DEV), 1)
    row_of_sums = lax.broadcasted_iota(jnp.int32, (1, OWNERS, 1), 1)
    entry_iota = lax.rem(row_of_sums, CHIPS) * NC + row_of_sums // CHIPS
    sum_row = lax.broadcasted_iota(jnp.int32, (LANES, 1), 0)
    is_count = lax.rem(sum_row, DSUB + 1) == DSUB
    same = lax.broadcasted_iota(jnp.int32, (LANES, LANES), 0) == lax.broadcasted_iota(
        jnp.int32, (LANES, LANES), 1
    )
    lane_of_row = lax.broadcasted_iota(
        jnp.int32, (CHIPS_G, NC * CAP, LANES), 2
    ) == z * NC * CAP + lax.broadcasted_iota(jnp.int32, (CHIPS_G, NC * CAP, LANES), 1)
    unit = jnp.where(same, 1.0, 0.0).astype(BF)

    def group_copy(g, many):
        return pltpu.make_async_remote_copy(
            src_ref=outb.at[g, 0:many],
            dst_ref=inb.at[g, 0:many],
            send_sem=out_sem.at[g],
            recv_sem=in_sem.at[g],
            device_id=(sibling, x),
            device_id_type=MESH,
        )

    def ids_group_copy(g, many):
        return pltpu.make_async_remote_copy(
            src_ref=ids_in.at[g, 0:many],
            dst_ref=ids_in.at[g, 0:many],
            send_sem=ids_send.at[g],
            recv_sem=ids_recv.at[g],
            device_id=(sibling, x),
            device_id_type=MESH,
        )

    def pay_copy(g, dt):
        to = lax.rem(x + dt, NX)
        return pltpu.make_async_remote_copy(
            src_ref=pay_out.at[g, to],
            dst_ref=pay_in.at[g, :, pl.ds(pl.multiple_of(x * ROWS_G, ROWS_G), ROWS_G)],
            send_sem=pay_send.at[g, dt],
            recv_sem=pay_recv.at[g, dt],
            device_id=(me, to),
            device_id_type=MESH,
        )

    def store_copy(g, s):
        from_y = lax.rem(y - g + NY, NY)
        to = pl.multiple_of(s * (OWNERS * CAP) + from_y * ROWS_G, ROWS_G)
        return pltpu.make_async_copy(
            pay_in.at[g, 0:COLS, s * ROWS_G : (s + 1) * ROWS_G],
            store_hbm.at[:, pl.ds(to, ROWS_G)],
            store_sem.at[g, s],
        )

    def rotate_group(g):
        @pl.when(g == 0)
        def _():
            group_copy(0, CHIPS_G - 1).wait_recv()
            ids_group_copy(0, CHIPS_G - 1).wait_recv()

        @pl.when(g > 0)
        def _():
            group_copy(g, CHIPS_G).wait_recv()
            ids_group_copy(g, CHIPS_G).wait_recv()

        ids = jnp.where(lane_of_row, ids_in[g].astype(F32), 0.0)
        list_row = jnp.sum(ids, axis=2, keepdims=True).reshape(ROWS_G, 1).astype(jnp.int32) - 4
        chosen = jnp.where(list_row == list_iota, 1.0, 0.0).astype(BF)
        for part in range(2):
            cut = slice(part * HALF, (part + 1) * HALF)
            picked = jnp.dot(chosen, cent[:, cut], preferred_element_type=F32)
            rows = inb[g, :, :, cut].astype(F32).reshape(ROWS_G, HALF)
            res[:, cut] = (rows - picked).astype(BF)
        code_tile = inb[g, :, :, D:MW].reshape(ROWS_G, LANES)
        code_rows[...] = lax.dot_general(unit, code_tile, NT, preferred_element_type=F32).astype(BF)
        own = pl.ds(pl.multiple_of(x * ROWS_G, ROWS_G), ROWS_G)
        for dt in (2, 1, 3, 0):
            t = lax.rem(x + dt, NX)
            turned = lax.dot_general(rot[t], res[...], NT, preferred_element_type=F32).astype(BF)
            mine = code_rows[pl.ds(pl.multiple_of(t * SUBS_DEV, SUBS_DEV), SUBS_DEV), :]
            if dt:
                pay_out[g, t, 0:COLS, :] = turned
                pay_out[g, t, COLS:PAY, :] = mine
                pay_copy(g, dt).start()
            else:
                pay_in[g, 0:COLS, own] = turned
                pay_in[g, COLS:PAY, own] = mine

    subspace = lane_iota // (DSUB + 1)

    def count_group(g, after):
        for dt in range(1, NX):
            pay_copy(g, dt).wait_recv()
        for s in range(NX):
            store_copy(g, s).start()
        upper = (pay_in[g, COLS:PAY, :].astype(F32).astype(jnp.int32) - 1) >> 2
        for part, (first, many) in enumerate(zip(FIRST, SPLIT)):
            value = jnp.dot(
                spread[part * LANES : (part + 1) * LANES, :], pay_in[g], preferred_element_type=F32
            )
            value = jnp.where(is_count, 1.0, value)
            lower = jnp.dot(
                spread[PW + part * LANES : PW + (part + 1) * LANES, :],
                pay_in[g],
                preferred_element_type=F32,
            )
            lower = (lower.astype(jnp.int32) - 1) & 3
            for lo in range(4):
                vals[lo * LANES : (lo + 1) * LANES, :] = jnp.where(lower == lo, value, 0.0).astype(
                    BF
                )
            ones = jnp.where(upper[first : first + many][:, None, :] == entry_iota, 1.0, 0.0)
            hot[0 : many * OWNERS, :] = ones.astype(BF).reshape(many * OWNERS, NX * ROWS_G)
            acc[part, 0 : many * OWNERS, :] += lax.dot_general(
                hot[0 : many * OWNERS, :], vals[...], NT, preferred_element_type=F32
            )
            after(part, many)

    acc[...] = jnp.zeros_like(acc)

    def both(g, carry):
        rotate_group(g)

        @pl.when(g > 0)
        def _():
            count_group(g - 1, lambda part, many: None)

        return carry

    lax.fori_loop(0, GROUPS, both, 0)

    def pair_copy(part):
        return pltpu.make_async_remote_copy(
            src_ref=sum_out.at[part, 1 - core],
            dst_ref=sum_pair.at[part],
            send_sem=pair_send.at[part],
            recv_sem=pair_recv.at[part],
            device_id=(sibling, x),
            device_id_type=MESH,
        )

    def finish_part(part, many):
        for lo in range(4):
            cut = slice(lo * LANES, (lo + 1) * LANES)
            total = jnp.zeros((OWNERS, LANES), F32)
            for i in range(many):
                total = jnp.where(
                    subspace == i, acc[part, i * OWNERS : (i + 1) * OWNERS, cut], total
                )
            sum_out[part, :, :, lo, :] = total.reshape(NC, CHIPS, LANES)
        pair_copy(part).start()

    count_group(GROUPS - 1, finish_part)
    for part in range(len(SPLIT)):
        pair_copy(part).wait_recv()
        sum_mid[:, part * 4 : part * 4 + 4, :] = sum_out[part, core] + sum_pair[part]

    def send_sum(k, carry):
        pltpu.make_async_remote_copy(
            src_ref=sum_mid.at[lax.rem(chip + k, CHIPS)],
            dst_ref=sum_in.at[k],
            send_sem=sum_send,
            recv_sem=sum_recv,
            device_id=(peer_of(k), x),
            device_id_type=MESH,
        ).start()
        return carry

    lax.fori_loop(1, CHIPS, send_sum, 0)
    sum_in[0] = sum_mid[chip]
    all_sums = pltpu.make_async_remote_copy(
        src_ref=sum_mid.at[1:CHIPS],
        dst_ref=sum_in.at[1:CHIPS],
        send_sem=sum_send,
        recv_sem=sum_recv,
        device_id=(sibling, x),
        device_id_type=MESH,
    )
    all_sums.wait_recv()
    total = jnp.sum(sum_in[...], axis=0)
    high = jnp.concatenate([total[part * 4 : part * 4 + 4] for part in range(len(SPLIT))], axis=1)
    terms = []
    for _ in range(3):
        term = high.astype(BF).astype(F32)
        terms.append(term)
        high = high - term
    placed = jnp.dot(
        jnp.concatenate(terms, axis=0).astype(BF), back[...], preferred_element_type=F32
    )
    placed = (placed[8:12] + placed[4:8]) + placed[0:4]
    sums, counts = placed[:, 0:COLS], placed[:, PW : PW + COLS]
    book_ref[...] = (sums + ANCHOR * old[...]) / (counts + ANCHOR)

    for swap in swaps:
        swap.wait_send()
    group_copy(0, CHIPS_G - 1).wait_send()
    ids_group_copy(0, CHIPS_G - 1).wait_send()
    for g in range(1, GROUPS):
        group_copy(g, CHIPS_G).wait_send()
        ids_group_copy(g, CHIPS_G).wait_send()
    for copy in [to_right, to_left, on_right, on_left] + shared:
        copy.wait_send()
    for g in range(GROUPS):
        for dt in range(1, NX):
            pay_copy(g, dt).wait_send()
    for part in range(len(SPLIT)):
        pair_copy(part).wait_send()
    all_sums.wait_send()
    for g in range(GROUPS):
        for s in range(NX):
            store_copy(g, s).wait()


def shards(embeddings, coarse_list_index, slots, codes, centroids, rotation, old_codebook):
    spread, back = layout_tables()
    vmem = pl.BlockSpec(memory_space=pltpu.VMEM)
    anywhere = pl.BlockSpec(memory_space=pl.ANY)
    dma = pltpu.SemaphoreType.DMA
    store, book = pl.pallas_call(
        kernel,
        out_shape=(
            jax.ShapeDtypeStruct((COLS, OWNERS * NX * CAP), BF),
            jax.ShapeDtypeStruct((CENT // OWNERS, COLS), F32),
        ),
        in_specs=[anywhere] * 9,
        out_specs=(anywhere, vmem),
        scratch_shapes=[
            pltpu.VMEM((NC * ROW_DEV, MW), BF),
            pltpu.VMEM((NC, 1, ROW_DEV), jnp.int32),
            pltpu.VMEM((NC, 1, ROW_DEV), jnp.int32),
            pltpu.VMEM((NC * ROW_DEV, LANES), jnp.int32),
            pltpu.VMEM((LIST_DEV, D), BF),
            pltpu.VMEM((NX, COLS, D), BF),
            pltpu.VMEM((CENT // OWNERS, COLS), F32),
            pltpu.VMEM((2 * PW, PAY), BF),
            pltpu.VMEM((PW, 2 * PW), BF),
            pltpu.VMEM((GROUPS, CHIPS_G, NC * CAP, MW), BF),
            pltpu.VMEM((GROUPS, CHIPS_G, NC * CAP, MW), BF),
            pltpu.VMEM((GROUPS, 1, LANES), jnp.int32),
            pltpu.VMEM((GROUPS, CHIPS_G, 1, LANES), jnp.int32),
            pltpu.VMEM((ROWS_G, D), BF),
            pltpu.VMEM((LANES, ROWS_G), BF),
            pltpu.VMEM((GROUPS, NX, PAY, ROWS_G), BF),
            pltpu.VMEM((GROUPS, PAY, NX * ROWS_G), BF),
            pltpu.VMEM((SPLIT[0] * OWNERS, NX * ROWS_G), BF),
            pltpu.VMEM((4 * LANES, NX * ROWS_G), BF),
            pltpu.VMEM((len(SPLIT), SPLIT[0] * OWNERS, 4 * LANES), F32),
            pltpu.VMEM((len(SPLIT), NC, CHIPS, 4, LANES), F32),
            pltpu.VMEM((len(SPLIT), CHIPS, 4, LANES), F32),
            pltpu.VMEM((CHIPS, 12, LANES), F32),
            pltpu.VMEM((CHIPS, 12, LANES), F32),
            dma((9,)),
            dma((4,)),
            dma((4,)),
            dma((GROUPS,)),
            dma((GROUPS,)),
            dma((GROUPS,)),
            dma((GROUPS,)),
            dma((7,)),
            dma((7,)),
            dma((GROUPS, NX)),
            dma((GROUPS, NX)),
            dma((1,)),
            dma((len(SPLIT),)),
            dma((len(SPLIT),)),
            dma(()),
            dma(()),
            dma((GROUPS, NX)),
        ],
        compiler_params=pltpu.CompilerParams(
            collective_id=0, has_side_effects=True, vmem_limit_bytes=56 * 2**20
        ),
    )(
        embeddings,
        coarse_list_index.reshape(1, ROW_DEV),
        slots.reshape(1, ROW_DEV),
        codes,
        centroids,
        rotation.T,
        old_codebook,
        jnp.asarray(spread, BF),
        jnp.asarray(back, BF),
    )
    return store.T, book


def solution(mesh):
    return jax.shard_map(
        shards,
        mesh=mesh,
        in_specs=(
            P(("list", "sub"), None),
            P(("list", "sub")),
            P(("list", "sub")),
            P(("list", "sub"), None),
            P("list", None),
            P(None, "sub"),
            P("list", "sub"),
        ),
        out_specs=(P("list", "sub"), P("list", "sub")),
        check_vma=False,
    )
```

```python
import functools

import jax
import jax.numpy as jnp
import numpy as np
from jax import lax
from jax.experimental import pallas as pl
from jax.experimental.pallas import tpu as pltpu
from jax.sharding import PartitionSpec as P

MESH = pl.DeviceIdType.MESH
NY, NZ, NC, NX = 4, 8, 2, 4
OWNERS = NY * NZ * NC
ROW_DEV = 256
CAP = 8
D = 1280
HALF = D // 2
COLS = D // NX
CENT = 256
LIST_DEV = 1024
SUBS_DEV = 32
DSUB = 10
GROUPS = 4
LAST = GROUPS - 1
CHIPS_G = 8
CHIPS = NY * NZ
ROWS_G = CHIPS_G * NC * CAP
MW = D + 128
PW = 384
PAY = COLS + SUBS_DEV
NT = (((1,), (1,)), ((), ()))
LANES = 128
SPLIT = (11, 11, 10)
FIRST = (0, 11, 22)
ANCHOR = 64.0
BF = jnp.bfloat16
F32 = jnp.float32


def layout_tables():
    spread = np.zeros((2 * PW, PAY), np.float32)
    back = np.zeros((PW, 2 * PW), np.float32)
    for g, (first, many) in enumerate(zip(FIRST, SPLIT)):
        for i in range(many):
            m = first + i
            for d in range(DSUB + 1):
                lane = i * (DSUB + 1) + d
                spread[PW + g * LANES + lane, COLS + m] = 1
                if d < DSUB:
                    spread[g * LANES + lane, m * DSUB + d] = 1
                    back[g * LANES + lane, m * DSUB + d] = 1
                    back[g * LANES + i * (DSUB + 1) + DSUB, PW + m * DSUB + d] = 1
    return spread, back


def kernel(
    emb_hbm,
    idx_hbm,
    slot_hbm,
    codes_hbm,
    cent_hbm,
    rot_hbm,
    old_hbm,
    spread_hbm,
    back_hbm,
    store_hbm,
    book_ref,
    emb,
    idx,
    slot,
    codes,
    cent,
    rot,
    old,
    spread,
    back,
    outb,
    inb,
    ids_out,
    ids_in,
    res,
    code_rows,
    pay_out,
    pay_in,
    hot,
    vals,
    acc,
    sum_out,
    sum_pair,
    sum_mid,
    sum_in,
    load_sem,
    swap_send,
    swap_recv,
    out_sem,
    in_sem,
    ids_send,
    ids_recv,
    rot_send,
    rot_recv,
    pay_send,
    pay_recv,
    own_sem,
    pair_send,
    pair_recv,
    sum_send,
    sum_recv,
    store_sem,
):
    me = lax.axis_index("list")
    x = lax.axis_index("sub")
    core = lax.rem(me, NC)
    chip = me // NC
    z = lax.rem(chip, NZ)
    y = chip // NZ
    sibling = me + 1 - 2 * core
    right, left = lax.rem(x + 1, NX), lax.rem(x + NX - 1, NX)
    across = lax.rem(x + 2, NX)

    own_rows = pl.ds(pl.multiple_of(core * ROW_DEV, ROW_DEV), ROW_DEV)
    sources = [
        (emb_hbm, emb.at[own_rows, 0:D]),
        (idx_hbm, idx.at[core]),
        (slot_hbm, slot.at[core]),
        (codes_hbm, codes.at[own_rows, :]),
    ]
    loads = [
        pltpu.make_async_copy(src, dst, load_sem.at[i]) for i, (src, dst) in enumerate(sources)
    ]
    later = [(cent_hbm, cent), (rot_hbm, rot.at[x]), (spread_hbm, spread), (back_hbm, back)]
    later.append((old_hbm, old))
    loads += [
        pltpu.make_async_copy(src, dst, load_sem.at[4 + i]) for i, (src, dst) in enumerate(later)
    ]
    for load in loads[:4]:
        load.start()

    barrier = pltpu.get_barrier_semaphore()

    def peer_of(k):
        return lax.rem(chip + k, CHIPS) * NC + core

    def greet(k, carry):
        pl.semaphore_signal(barrier, inc=1, device_id=(peer_of(k), x), device_id_type=MESH)
        return carry

    lax.fori_loop(1, CHIPS, greet, 0)
    pl.semaphore_signal(barrier, inc=1, device_id=(sibling, x), device_id_type=MESH)
    for k in range(1, NX):
        pl.semaphore_signal(
            barrier, inc=1, device_id=(me, lax.rem(x + k, NX)), device_id_type=MESH
        )
    pl.semaphore_wait(barrier, CHIPS + NX - 1)

    swaps = [
        pltpu.make_async_remote_copy(
            src_ref=src,
            dst_ref=dst,
            send_sem=swap_send.at[i],
            recv_sem=swap_recv.at[i],
            device_id=(sibling, x),
            device_id_type=MESH,
        )
        for i, (src, dst) in enumerate(sources)
    ]
    for swap in swaps:
        swap.start()

    half = COLS // 2
    half_rows = pl.ds(pl.multiple_of(core * half, half), half)
    quarter_a = pl.ds(pl.multiple_of(core * half, half // 2), half // 2)
    quarter_b = pl.ds(pl.multiple_of(core * half + half // 2, half // 2), half // 2)

    def rot_copy(src, block, rows, number, l, s):
        return pltpu.make_async_remote_copy(
            src_ref=src,
            dst_ref=rot.at[block, rows, :],
            send_sem=rot_send.at[number],
            recv_sem=rot_recv.at[number],
            device_id=(l, s),
            device_id_type=MESH,
        )

    to_right = rot_copy(rot_hbm.at[half_rows, :], x, half_rows, 0, me, right)
    to_left = rot_copy(rot_hbm.at[half_rows, :], x, half_rows, 1, me, left)
    to_right.start()
    to_left.start()
    for load in loads[4:]:
        load.start()

    for load in loads[:4]:
        load.wait()
    for swap in swaps:
        swap.wait_recv()
    emb[:, D:MW] = (codes[...] + 1).astype(F32).astype(BF)
    keys, uppers, lowers = [], [], []
    for c in range(NC):
        list_id = idx[c]
        owner = list_id // LIST_DEV
        key = (owner // NC * NC + c) * CAP + slot[c]
        keys.append(jnp.where(lax.rem(owner, NC) == core, key, -1))
        local = lax.rem(list_id, LIST_DEV)
        uppers.append((local // 4 + 1).astype(F32).astype(BF))
        lowers.append(lax.rem(local, 4).astype(F32).astype(BF))
    key = jnp.concatenate(keys, axis=1)
    upper_id = jnp.concatenate(uppers, axis=1)
    lower_id = jnp.concatenate(lowers, axis=1)
    row_iota = lax.broadcasted_iota(jnp.int32, (ROWS_G, 1), 0)
    lane_iota = lax.broadcasted_iota(jnp.int32, (1, LANES), 1)

    def row_copy(g, l, to_z):
        return pltpu.make_async_remote_copy(
            src_ref=outb.at[g, to_z],
            dst_ref=inb.at[g, z],
            send_sem=out_sem.at[g],
            recv_sem=in_sem.at[g],
            device_id=(l, x),
            device_id_type=MESH,
        )

    def ids_copy(g, l):
        return pltpu.make_async_remote_copy(
            src_ref=ids_out.at[g],
            dst_ref=ids_in.at[g, z],
            send_sem=ids_send.at[g],
            recv_sem=ids_recv.at[g],
            device_id=(l, x),
            device_id_type=MESH,
        )

    def far_first(k):
        return NZ // 2 + jnp.where(lax.rem(k, 2) == 1, -((k + 1) // 2), k // 2)

    def send_group(g, carry):
        to_y = lax.rem(y + g + 1, NY)
        place = jnp.where(to_y * ROWS_G + row_iota == key, 1.0, 0.0).astype(BF)
        ids = 4.0 * lax.dot_general(
            upper_id, place, NT, preferred_element_type=F32
        ) + lax.dot_general(lower_id, place, NT, preferred_element_type=F32)
        ids_out[g] = ids.astype(jnp.int32)
        made = jnp.dot(place, emb[...], preferred_element_type=F32)
        outb[g] = made.astype(BF).reshape(CHIPS_G, NC * CAP, MW)

        def send(k, carry):
            to_z = lax.rem(z + far_first(k), NZ)
            l = (to_y * NZ + to_z) * NC + core
            ids_copy(g, l).start()
            row_copy(g, l, to_z).start()
            return carry

        lax.fori_loop(0, jnp.where(g == LAST, CHIPS_G - 1, CHIPS_G), send, 0)
        return carry

    lax.fori_loop(0, GROUPS, send_group, 0)
    own_block = pltpu.make_async_copy(outb.at[LAST, z], inb.at[LAST, z], own_sem.at[0])
    own_block.start()
    ids_in[LAST, z] = ids_out[LAST]

    def to_sibling(block, number):
        copy = rot_copy(rot.at[block, half_rows, :], block, half_rows, number, sibling, x)
        copy.start()
        return copy

    to_right.wait_recv()
    on_right = rot_copy(rot.at[left, quarter_a, :], left, quarter_a, 2, me, right)
    on_right.start()
    to_left.wait_recv()
    on_left = rot_copy(rot.at[right, quarter_b, :], right, quarter_b, 3, me, left)
    on_left.start()
    shared = [to_sibling(left, 4), to_sibling(right, 5)]
    on_right.wait_recv()
    on_left.wait_recv()
    shared.append(to_sibling(across, 6))
    for load in loads[4:]:
        load.wait()
    own_block.wait()
    for copy in shared:
        copy.wait_recv()

    list_iota = lax.broadcasted_iota(jnp.int32, (1, LIST_DEV), 1)
    row_of_sums = lax.broadcasted_iota(jnp.int32, (1, OWNERS, 1), 1)
    entry_iota = lax.rem(row_of_sums, CHIPS) * NC + row_of_sums // CHIPS
    sum_row = lax.broadcasted_iota(jnp.int32, (LANES, 1), 0)
    is_count = lax.rem(sum_row, DSUB + 1) == DSUB
    same = lax.broadcasted_iota(jnp.int32, (LANES, LANES), 0) == lax.broadcasted_iota(
        jnp.int32, (LANES, LANES), 1
    )
    lane_of_row = lax.broadcasted_iota(
        jnp.int32, (CHIPS_G, NC * CAP, LANES), 2
    ) == z * NC * CAP + lax.broadcasted_iota(jnp.int32, (CHIPS_G, NC * CAP, LANES), 1)
    unit = jnp.where(same, 1.0, 0.0).astype(BF)

    def group_copy(g, many):
        return pltpu.make_async_remote_copy(
            src_ref=outb.at[g, 0:many],
            dst_ref=inb.at[g, 0:many],
            send_sem=out_sem.at[g],
            recv_sem=in_sem.at[g],
            device_id=(sibling, x),
            device_id_type=MESH,
        )

    def ids_group_copy(g, many):
        return pltpu.make_async_remote_copy(
            src_ref=ids_in.at[g, 0:many],
            dst_ref=ids_in.at[g, 0:many],
            send_sem=ids_send.at[g],
            recv_sem=ids_recv.at[g],
            device_id=(sibling, x),
            device_id_type=MESH,
        )

    def pay_copy(g, dt):
        to = lax.rem(x + dt, NX)
        return pltpu.make_async_remote_copy(
            src_ref=pay_out.at[g, to],
            dst_ref=pay_in.at[g, :, pl.ds(pl.multiple_of(x * ROWS_G, ROWS_G), ROWS_G)],
            send_sem=pay_send.at[g, dt],
            recv_sem=pay_recv.at[g, dt],
            device_id=(me, to),
            device_id_type=MESH,
        )

    def store_copy(g, s):
        from_y = lax.rem(y - g + NY - 1, NY)
        to = pl.multiple_of(s * (OWNERS * CAP) + from_y * ROWS_G, ROWS_G)
        return pltpu.make_async_copy(
            pay_in.at[g, 0:COLS, s * ROWS_G : (s + 1) * ROWS_G],
            store_hbm.at[:, pl.ds(to, ROWS_G)],
            store_sem.at[g, s],
        )

    def rotate_group(g):
        @pl.when(g == LAST)
        def _():
            group_copy(LAST, CHIPS_G - 1).wait_recv()
            ids_group_copy(LAST, CHIPS_G - 1).wait_recv()

        @pl.when(g < LAST)
        def _():
            group_copy(g, CHIPS_G).wait_recv()
            ids_group_copy(g, CHIPS_G).wait_recv()

        ids = jnp.where(lane_of_row, ids_in[g].astype(F32), 0.0)
        list_row = jnp.sum(ids, axis=2, keepdims=True).reshape(ROWS_G, 1).astype(jnp.int32) - 4
        chosen = jnp.where(list_row == list_iota, 1.0, 0.0).astype(BF)
        for part in range(2):
            cut = slice(part * HALF, (part + 1) * HALF)
            picked = jnp.dot(chosen, cent[:, cut], preferred_element_type=F32)
            rows = inb[g, :, :, cut].astype(F32).reshape(ROWS_G, HALF)
            res[:, cut] = (rows - picked).astype(BF)
        code_tile = inb[g, :, :, D:MW].reshape(ROWS_G, LANES)
        code_rows[...] = lax.dot_general(unit, code_tile, NT, preferred_element_type=F32).astype(BF)
        own = pl.ds(pl.multiple_of(x * ROWS_G, ROWS_G), ROWS_G)
        for dt in (2, 1, 3, 0):
            t = lax.rem(x + dt, NX)
            turned = lax.dot_general(rot[t], res[...], NT, preferred_element_type=F32).astype(BF)
            mine = code_rows[pl.ds(pl.multiple_of(t * SUBS_DEV, SUBS_DEV), SUBS_DEV), :]
            if dt:
                pay_out[g, t, 0:COLS, :] = turned
                pay_out[g, t, COLS:PAY, :] = mine
                pay_copy(g, dt).start()
            else:
                pay_in[g, 0:COLS, own] = turned
                pay_in[g, COLS:PAY, own] = mine

    subspace = lane_iota // (DSUB + 1)

    def count_group(g, after):
        for dt in range(1, NX):
            pay_copy(g, dt).wait_recv()
        for s in range(NX):
            store_copy(g, s).start()
        upper = (pay_in[g, COLS:PAY, :].astype(F32).astype(jnp.int32) - 1) >> 2
        for part, (first, many) in enumerate(zip(FIRST, SPLIT)):
            value = jnp.dot(
                spread[part * LANES : (part + 1) * LANES, :], pay_in[g], preferred_element_type=F32
            )
            value = jnp.where(is_count, 1.0, value)
            lower = jnp.dot(
                spread[PW + part * LANES : PW + (part + 1) * LANES, :],
                pay_in[g],
                preferred_element_type=F32,
            )
            lower = (lower.astype(jnp.int32) - 1) & 3
            for lo in range(4):
                vals[lo * LANES : (lo + 1) * LANES, :] = jnp.where(lower == lo, value, 0.0).astype(
                    BF
                )
            ones = jnp.where(upper[first : first + many][:, None, :] == entry_iota, 1.0, 0.0)
            hot[0 : many * OWNERS, :] = ones.astype(BF).reshape(many * OWNERS, NX * ROWS_G)
            acc[part, 0 : many * OWNERS, :] += lax.dot_general(
                hot[0 : many * OWNERS, :], vals[...], NT, preferred_element_type=F32
            )
            after(part, many)

    acc[...] = jnp.zeros_like(acc)

    def both(g, carry):
        rotate_group(g)

        @pl.when(g > 0)
        def _():
            count_group(g - 1, lambda part, many: None)

        return carry

    lax.fori_loop(0, GROUPS, both, 0)

    def pair_copy(part):
        return pltpu.make_async_remote_copy(
            src_ref=sum_out.at[part, 1 - core],
            dst_ref=sum_pair.at[part],
            send_sem=pair_send.at[part],
            recv_sem=pair_recv.at[part],
            device_id=(sibling, x),
            device_id_type=MESH,
        )

    def finish_part(part, many):
        for lo in range(4):
            cut = slice(lo * LANES, (lo + 1) * LANES)
            total = jnp.zeros((OWNERS, LANES), F32)
            for i in range(many):
                total = jnp.where(
                    subspace == i, acc[part, i * OWNERS : (i + 1) * OWNERS, cut], total
                )
            sum_out[part, :, :, lo, :] = total.reshape(NC, CHIPS, LANES)
        pair_copy(part).start()

    count_group(GROUPS - 1, finish_part)
    for part in range(len(SPLIT)):
        pair_copy(part).wait_recv()
        sum_mid[:, part * 4 : part * 4 + 4, :] = sum_out[part, core] + sum_pair[part]

    def send_sum(k, carry):
        to = lax.rem(y + k // NZ + 1, NY) * NZ + lax.rem(z + far_first(lax.rem(k, NZ)), NZ)
        pltpu.make_async_remote_copy(
            src_ref=sum_mid.at[to],
            dst_ref=sum_in.at[k],
            send_sem=sum_send,
            recv_sem=sum_recv,
            device_id=(to * NC + core, x),
            device_id_type=MESH,
        ).start()
        return carry

    lax.fori_loop(0, CHIPS - 1, send_sum, 0)
    sum_in[CHIPS - 1] = sum_mid[chip]
    all_sums = pltpu.make_async_remote_copy(
        src_ref=sum_mid.at[0 : CHIPS - 1],
        dst_ref=sum_in.at[0 : CHIPS - 1],
        send_sem=sum_send,
        recv_sem=sum_recv,
        device_id=(sibling, x),
        device_id_type=MESH,
    )
    all_sums.wait_recv()
    total = jnp.sum(sum_in[...], axis=0)
    high = jnp.concatenate([total[part * 4 : part * 4 + 4] for part in range(len(SPLIT))], axis=1)
    terms = []
    for _ in range(3):
        term = high.astype(BF).astype(F32)
        terms.append(term)
        high = high - term
    placed = jnp.dot(
        jnp.concatenate(terms, axis=0).astype(BF), back[...], preferred_element_type=F32
    )
    placed = (placed[8:12] + placed[4:8]) + placed[0:4]
    sums, counts = placed[:, 0:COLS], placed[:, PW : PW + COLS]
    book_ref[...] = (sums + ANCHOR * old[...]) / (counts + ANCHOR)

    for swap in swaps:
        swap.wait_send()
    group_copy(LAST, CHIPS_G - 1).wait_send()
    ids_group_copy(LAST, CHIPS_G - 1).wait_send()
    for g in range(LAST):
        group_copy(g, CHIPS_G).wait_send()
        ids_group_copy(g, CHIPS_G).wait_send()
    for copy in [to_right, to_left, on_right, on_left] + shared:
        copy.wait_send()
    for g in range(GROUPS):
        for dt in range(1, NX):
            pay_copy(g, dt).wait_send()
    for part in range(len(SPLIT)):
        pair_copy(part).wait_send()
    all_sums.wait_send()
    for g in range(GROUPS):
        for s in range(NX):
            store_copy(g, s).wait()


def shards(embeddings, coarse_list_index, slots, codes, centroids, rotation, old_codebook):
    spread, back = layout_tables()
    vmem = pl.BlockSpec(memory_space=pltpu.VMEM)
    anywhere = pl.BlockSpec(memory_space=pl.ANY)
    dma = pltpu.SemaphoreType.DMA
    store, book = pl.pallas_call(
        kernel,
        out_shape=(
            jax.ShapeDtypeStruct((COLS, OWNERS * NX * CAP), BF),
            jax.ShapeDtypeStruct((CENT // OWNERS, COLS), F32),
        ),
        in_specs=[anywhere] * 9,
        out_specs=(anywhere, vmem),
        scratch_shapes=[
            pltpu.VMEM((NC * ROW_DEV, MW), BF),
            pltpu.VMEM((NC, 1, ROW_DEV), jnp.int32),
            pltpu.VMEM((NC, 1, ROW_DEV), jnp.int32),
            pltpu.VMEM((NC * ROW_DEV, LANES), jnp.int32),
            pltpu.VMEM((LIST_DEV, D), BF),
            pltpu.VMEM((NX, COLS, D), BF),
            pltpu.VMEM((CENT // OWNERS, COLS), F32),
            pltpu.VMEM((2 * PW, PAY), BF),
            pltpu.VMEM((PW, 2 * PW), BF),
            pltpu.VMEM((GROUPS, CHIPS_G, NC * CAP, MW), BF),
            pltpu.VMEM((GROUPS, CHIPS_G, NC * CAP, MW), BF),
            pltpu.VMEM((GROUPS, 1, LANES), jnp.int32),
            pltpu.VMEM((GROUPS, CHIPS_G, 1, LANES), jnp.int32),
            pltpu.VMEM((ROWS_G, D), BF),
            pltpu.VMEM((LANES, ROWS_G), BF),
            pltpu.VMEM((GROUPS, NX, PAY, ROWS_G), BF),
            pltpu.VMEM((GROUPS, PAY, NX * ROWS_G), BF),
            pltpu.VMEM((SPLIT[0] * OWNERS, NX * ROWS_G), BF),
            pltpu.VMEM((4 * LANES, NX * ROWS_G), BF),
            pltpu.VMEM((len(SPLIT), SPLIT[0] * OWNERS, 4 * LANES), F32),
            pltpu.VMEM((len(SPLIT), NC, CHIPS, 4, LANES), F32),
            pltpu.VMEM((len(SPLIT), CHIPS, 4, LANES), F32),
            pltpu.VMEM((CHIPS, 12, LANES), F32),
            pltpu.VMEM((CHIPS, 12, LANES), F32),
            dma((9,)),
            dma((4,)),
            dma((4,)),
            dma((GROUPS,)),
            dma((GROUPS,)),
            dma((GROUPS,)),
            dma((GROUPS,)),
            dma((7,)),
            dma((7,)),
            dma((GROUPS, NX)),
            dma((GROUPS, NX)),
            dma((1,)),
            dma((len(SPLIT),)),
            dma((len(SPLIT),)),
            dma(()),
            dma(()),
            dma((GROUPS, NX)),
        ],
        compiler_params=pltpu.CompilerParams(
            collective_id=0, has_side_effects=True, vmem_limit_bytes=56 * 2**20
        ),
    )(
        embeddings,
        coarse_list_index.reshape(1, ROW_DEV),
        slots.reshape(1, ROW_DEV),
        codes,
        centroids,
        rotation.T,
        old_codebook,
        jnp.asarray(spread, BF),
        jnp.asarray(back, BF),
    )
    return store.T, book


def solution(mesh):
    return jax.shard_map(
        shards,
        mesh=mesh,
        in_specs=(
            P(("list", "sub"), None),
            P(("list", "sub")),
            P(("list", "sub")),
            P(("list", "sub"), None),
            P("list", None),
            P(None, "sub"),
            P("list", "sub"),
        ),
        out_specs=(P("list", "sub"), P("list", "sub")),
        check_vma=False,
    )
```

```python
import functools

import jax
import jax.numpy as jnp
import numpy as np
from jax import lax
from jax.experimental import pallas as pl
from jax.experimental.pallas import tpu as pltpu
from jax.sharding import PartitionSpec as P

MESH = pl.DeviceIdType.MESH
NY, NZ, NC, NX = 4, 8, 2, 4
OWNERS = NY * NZ * NC
ROW_DEV = 256
CAP = 8
D = 1280
HALF = D // 2
COLS = D // NX
CENT = 256
LIST_DEV = 1024
SUBS_DEV = 32
DSUB = 10
GROUPS = 4
LAST = GROUPS - 1
CHIPS_G = 8
CHIPS = NY * NZ
ROWS_G = CHIPS_G * NC * CAP
MW = D + 128
PW = 384
PAY = COLS + SUBS_DEV
NT = (((1,), (1,)), ((), ()))
LANES = 128
SPLIT = (11, 11, 10)
FIRST = (0, 11, 22)
ANCHOR = 64.0
BF = jnp.bfloat16
F32 = jnp.float32


def layout_tables():
    spread = np.zeros((2 * PW, PAY), np.float32)
    back = np.zeros((PW, 2 * PW), np.float32)
    for g, (first, many) in enumerate(zip(FIRST, SPLIT)):
        for i in range(many):
            m = first + i
            for d in range(DSUB + 1):
                lane = i * (DSUB + 1) + d
                spread[PW + g * LANES + lane, COLS + m] = 1
                if d < DSUB:
                    spread[g * LANES + lane, m * DSUB + d] = 1
                    back[g * LANES + lane, m * DSUB + d] = 1
                    back[g * LANES + i * (DSUB + 1) + DSUB, PW + m * DSUB + d] = 1
    return spread, back


def kernel(
    emb_hbm,
    idx_hbm,
    slot_hbm,
    codes_hbm,
    cent_hbm,
    rot_hbm,
    old_hbm,
    spread_hbm,
    back_hbm,
    store_hbm,
    book_ref,
    emb,
    idx,
    slot,
    codes,
    cent,
    rot,
    old,
    spread,
    back,
    outb,
    inb,
    ids_out,
    ids_in,
    res,
    code_rows,
    pay_out,
    pay_in,
    hot,
    vals,
    acc,
    sum_out,
    sum_pair,
    sum_mid,
    sum_in,
    load_sem,
    swap_send,
    swap_recv,
    out_sem,
    in_sem,
    ids_send,
    ids_recv,
    rot_send,
    rot_recv,
    pay_send,
    pay_recv,
    own_sem,
    pair_send,
    pair_recv,
    sum_send,
    sum_recv,
    store_sem,
):
    me = lax.axis_index("list")
    x = lax.axis_index("sub")
    core = lax.rem(me, NC)
    chip = me // NC
    z = lax.rem(chip, NZ)
    y = chip // NZ
    sibling = me + 1 - 2 * core
    right, left = lax.rem(x + 1, NX), lax.rem(x + NX - 1, NX)
    across = lax.rem(x + 2, NX)

    own_rows = pl.ds(pl.multiple_of(core * ROW_DEV, ROW_DEV), ROW_DEV)
    sources = [
        (emb_hbm, emb.at[own_rows, 0:D]),
        (idx_hbm, idx.at[core]),
        (slot_hbm, slot.at[core]),
        (codes_hbm, codes.at[own_rows, :]),
    ]
    loads = [
        pltpu.make_async_copy(src, dst, load_sem.at[i]) for i, (src, dst) in enumerate(sources)
    ]
    later = [(cent_hbm, cent), (rot_hbm, rot.at[x]), (spread_hbm, spread), (back_hbm, back)]
    later.append((old_hbm, old))
    loads += [
        pltpu.make_async_copy(src, dst, load_sem.at[4 + i]) for i, (src, dst) in enumerate(later)
    ]
    for load in loads[:4]:
        load.start()

    barrier = pltpu.get_barrier_semaphore()

    def peer_of(k):
        return lax.rem(chip + k, CHIPS) * NC + core

    def greet(k, carry):
        pl.semaphore_signal(barrier, inc=1, device_id=(peer_of(k), x), device_id_type=MESH)
        return carry

    lax.fori_loop(1, CHIPS, greet, 0)
    pl.semaphore_signal(barrier, inc=1, device_id=(sibling, x), device_id_type=MESH)
    for k in range(1, NX):
        pl.semaphore_signal(
            barrier, inc=1, device_id=(me, lax.rem(x + k, NX)), device_id_type=MESH
        )
    pl.semaphore_wait(barrier, CHIPS + NX - 1)

    swaps = [
        pltpu.make_async_remote_copy(
            src_ref=src,
            dst_ref=dst,
            send_sem=swap_send.at[i],
            recv_sem=swap_recv.at[i],
            device_id=(sibling, x),
            device_id_type=MESH,
        )
        for i, (src, dst) in enumerate(sources)
    ]
    for swap in swaps:
        swap.start()

    half = COLS // 2
    half_rows = pl.ds(pl.multiple_of(core * half, half), half)
    quarter_a = pl.ds(pl.multiple_of(core * half, half // 2), half // 2)
    quarter_b = pl.ds(pl.multiple_of(core * half + half // 2, half // 2), half // 2)

    def rot_copy(src, block, rows, number, l, s):
        return pltpu.make_async_remote_copy(
            src_ref=src,
            dst_ref=rot.at[block, rows, :],
            send_sem=rot_send.at[number],
            recv_sem=rot_recv.at[number],
            device_id=(l, s),
            device_id_type=MESH,
        )

    to_right = rot_copy(rot_hbm.at[half_rows, :], x, half_rows, 0, me, right)
    to_left = rot_copy(rot_hbm.at[half_rows, :], x, half_rows, 1, me, left)
    to_right.start()
    to_left.start()
    for load in loads[4:]:
        load.start()

    for load in loads[:4]:
        load.wait()
    for swap in swaps:
        swap.wait_recv()
    emb[:, D:MW] = (codes[...] + 1).astype(F32).astype(BF)
    keys, uppers, lowers = [], [], []
    for c in range(NC):
        list_id = idx[c]
        owner = list_id // LIST_DEV
        key = (owner // NC * NC + c) * CAP + slot[c]
        keys.append(jnp.where(lax.rem(owner, NC) == core, key, -1))
        local = lax.rem(list_id, LIST_DEV)
        uppers.append((local // 4 + 1).astype(F32).astype(BF))
        lowers.append(lax.rem(local, 4).astype(F32).astype(BF))
    key = jnp.concatenate(keys, axis=1)
    upper_id = jnp.concatenate(uppers, axis=1)
    lower_id = jnp.concatenate(lowers, axis=1)
    row_iota = lax.broadcasted_iota(jnp.int32, (ROWS_G, 1), 0)
    lane_iota = lax.broadcasted_iota(jnp.int32, (1, LANES), 1)

    def row_copy(g, l, to_z):
        return pltpu.make_async_remote_copy(
            src_ref=outb.at[g, to_z],
            dst_ref=inb.at[g, z],
            send_sem=out_sem.at[g],
            recv_sem=in_sem.at[g],
            device_id=(l, x),
            device_id_type=MESH,
        )

    def ids_copy(g, l):
        return pltpu.make_async_remote_copy(
            src_ref=ids_out.at[g],
            dst_ref=ids_in.at[g, z],
            send_sem=ids_send.at[g],
            recv_sem=ids_recv.at[g],
            device_id=(l, x),
            device_id_type=MESH,
        )

    def far_first(k):
        return NZ // 2 + jnp.where(lax.rem(k, 2) == 1, -((k + 1) // 2), k // 2)

    def send_group(g, carry):
        to_y = lax.rem(y + g + 1, NY)
        place = jnp.where(to_y * ROWS_G + row_iota == key, 1.0, 0.0).astype(BF)
        made = jnp.dot(place, emb[...], preferred_element_type=F32)
        outb[g] = made.astype(BF).reshape(CHIPS_G, NC * CAP, MW)
        ids = 4.0 * lax.dot_general(
            upper_id, place, NT, preferred_element_type=F32
        ) + lax.dot_general(lower_id, place, NT, preferred_element_type=F32)
        ids_out[g] = ids.astype(jnp.int32)

        def send(k, carry):
            to_z = lax.rem(z + far_first(k), NZ)
            l = (to_y * NZ + to_z) * NC + core
            row_copy(g, l, to_z).start()
            ids_copy(g, l).start()
            return carry

        lax.fori_loop(0, jnp.where(g == LAST, CHIPS_G - 1, CHIPS_G), send, 0)
        return carry

    lax.fori_loop(0, GROUPS, send_group, 0)
    own_block = pltpu.make_async_copy(outb.at[LAST, z], inb.at[LAST, z], own_sem.at[0])
    own_block.start()
    ids_in[LAST, z] = ids_out[LAST]

    def to_sibling(block, number):
        copy = rot_copy(rot.at[block, half_rows, :], block, half_rows, number, sibling, x)
        copy.start()
        return copy

    to_right.wait_recv()
    on_right = rot_copy(rot.at[left, quarter_a, :], left, quarter_a, 2, me, right)
    on_right.start()
    to_left.wait_recv()
    on_left = rot_copy(rot.at[right, quarter_b, :], right, quarter_b, 3, me, left)
    on_left.start()
    shared = [to_sibling(left, 4), to_sibling(right, 5)]
    on_right.wait_recv()
    on_left.wait_recv()
    shared.append(to_sibling(across, 6))
    for load in loads[4:]:
        load.wait()
    own_block.wait()
    for copy in shared:
        copy.wait_recv()

    list_iota = lax.broadcasted_iota(jnp.int32, (1, LIST_DEV), 1)
    row_of_sums = lax.broadcasted_iota(jnp.int32, (1, OWNERS, 1), 1)
    entry_iota = lax.rem(row_of_sums, CHIPS) * NC + row_of_sums // CHIPS
    sum_row = lax.broadcasted_iota(jnp.int32, (LANES, 1), 0)
    is_count = lax.rem(sum_row, DSUB + 1) == DSUB
    same = lax.broadcasted_iota(jnp.int32, (LANES, LANES), 0) == lax.broadcasted_iota(
        jnp.int32, (LANES, LANES), 1
    )
    lane_of_row = lax.broadcasted_iota(
        jnp.int32, (CHIPS_G, NC * CAP, LANES), 2
    ) == z * NC * CAP + lax.broadcasted_iota(jnp.int32, (CHIPS_G, NC * CAP, LANES), 1)
    unit = jnp.where(same, 1.0, 0.0).astype(BF)

    def group_copy(g, many):
        return pltpu.make_async_remote_copy(
            src_ref=outb.at[g, 0:many],
            dst_ref=inb.at[g, 0:many],
            send_sem=out_sem.at[g],
            recv_sem=in_sem.at[g],
            device_id=(sibling, x),
            device_id_type=MESH,
        )

    def ids_group_copy(g, many):
        return pltpu.make_async_remote_copy(
            src_ref=ids_in.at[g, 0:many],
            dst_ref=ids_in.at[g, 0:many],
            send_sem=ids_send.at[g],
            recv_sem=ids_recv.at[g],
            device_id=(sibling, x),
            device_id_type=MESH,
        )

    def pay_copy(g, dt):
        to = lax.rem(x + dt, NX)
        return pltpu.make_async_remote_copy(
            src_ref=pay_out.at[g, to],
            dst_ref=pay_in.at[g, :, pl.ds(pl.multiple_of(x * ROWS_G, ROWS_G), ROWS_G)],
            send_sem=pay_send.at[g, dt],
            recv_sem=pay_recv.at[g, dt],
            device_id=(me, to),
            device_id_type=MESH,
        )

    def store_copy(g, s):
        from_y = lax.rem(y - g + NY - 1, NY)
        to = pl.multiple_of(s * (OWNERS * CAP) + from_y * ROWS_G, ROWS_G)
        return pltpu.make_async_copy(
            pay_in.at[g, 0:COLS, s * ROWS_G : (s + 1) * ROWS_G],
            store_hbm.at[:, pl.ds(to, ROWS_G)],
            store_sem.at[g, s],
        )

    def rotate_group(g):
        @pl.when(g == LAST)
        def _():
            group_copy(LAST, CHIPS_G - 1).wait_recv()
            ids_group_copy(LAST, CHIPS_G - 1).wait_recv()

        @pl.when(g < LAST)
        def _():
            group_copy(g, CHIPS_G).wait_recv()
            ids_group_copy(g, CHIPS_G).wait_recv()

        ids = jnp.where(lane_of_row, ids_in[g].astype(F32), 0.0)
        list_row = jnp.sum(ids, axis=2, keepdims=True).reshape(ROWS_G, 1).astype(jnp.int32) - 4
        chosen = jnp.where(list_row == list_iota, 1.0, 0.0).astype(BF)
        for part in range(2):
            cut = slice(part * HALF, (part + 1) * HALF)
            picked = jnp.dot(chosen, cent[:, cut], preferred_element_type=F32)
            rows = inb[g, :, :, cut].astype(F32).reshape(ROWS_G, HALF)
            res[:, cut] = (rows - picked).astype(BF)
        code_tile = inb[g, :, :, D:MW].reshape(ROWS_G, LANES)
        code_rows[...] = lax.dot_general(unit, code_tile, NT, preferred_element_type=F32).astype(BF)
        own = pl.ds(pl.multiple_of(x * ROWS_G, ROWS_G), ROWS_G)
        for dt in (2, 1, 3, 0):
            t = lax.rem(x + dt, NX)
            turned = lax.dot_general(rot[t], res[...], NT, preferred_element_type=F32).astype(BF)
            mine = code_rows[pl.ds(pl.multiple_of(t * SUBS_DEV, SUBS_DEV), SUBS_DEV), :]
            if dt:
                pay_out[g, t, 0:COLS, :] = turned
                pay_out[g, t, COLS:PAY, :] = mine
                pay_copy(g, dt).start()
            else:
                pay_in[g, 0:COLS, own] = turned
                pay_in[g, COLS:PAY, own] = mine

    subspace = lane_iota // (DSUB + 1)

    def count_group(g, after):
        for dt in range(1, NX):
            pay_copy(g, dt).wait_recv()
        for s in range(NX):
            store_copy(g, s).start()
        upper = (pay_in[g, COLS:PAY, :].astype(F32).astype(jnp.int32) - 1) >> 2
        for part, (first, many) in enumerate(zip(FIRST, SPLIT)):
            value = jnp.dot(
                spread[part * LANES : (part + 1) * LANES, :], pay_in[g], preferred_element_type=F32
            )
            value = jnp.where(is_count, 1.0, value)
            lower = jnp.dot(
                spread[PW + part * LANES : PW + (part + 1) * LANES, :],
                pay_in[g],
                preferred_element_type=F32,
            )
            lower = (lower.astype(jnp.int32) - 1) & 3
            for lo in range(4):
                vals[lo * LANES : (lo + 1) * LANES, :] = jnp.where(lower == lo, value, 0.0).astype(
                    BF
                )
            ones = jnp.where(upper[first : first + many][:, None, :] == entry_iota, 1.0, 0.0)
            hot[0 : many * OWNERS, :] = ones.astype(BF).reshape(many * OWNERS, NX * ROWS_G)
            acc[part, 0 : many * OWNERS, :] += lax.dot_general(
                hot[0 : many * OWNERS, :], vals[...], NT, preferred_element_type=F32
            )
            after(part, many)

    acc[...] = jnp.zeros_like(acc)

    def both(g, carry):
        rotate_group(g)

        @pl.when(g > 0)
        def _():
            count_group(g - 1, lambda part, many: None)

        return carry

    lax.fori_loop(0, GROUPS, both, 0)

    def pair_copy(part):
        return pltpu.make_async_remote_copy(
            src_ref=sum_out.at[part, 1 - core],
            dst_ref=sum_pair.at[part],
            send_sem=pair_send.at[part],
            recv_sem=pair_recv.at[part],
            device_id=(sibling, x),
            device_id_type=MESH,
        )

    def finish_part(part, many):
        for lo in range(4):
            cut = slice(lo * LANES, (lo + 1) * LANES)
            total = jnp.zeros((OWNERS, LANES), F32)
            for i in range(many):
                total = jnp.where(
                    subspace == i, acc[part, i * OWNERS : (i + 1) * OWNERS, cut], total
                )
            sum_out[part, :, :, lo, :] = total.reshape(NC, CHIPS, LANES)
        pair_copy(part).start()

    count_group(GROUPS - 1, finish_part)
    for part in range(len(SPLIT)):
        pair_copy(part).wait_recv()
        sum_mid[:, part * 4 : part * 4 + 4, :] = sum_out[part, core] + sum_pair[part]

    def send_sum(k, carry):
        to = lax.rem(y + k // NZ + 1, NY) * NZ + lax.rem(z + far_first(lax.rem(k, NZ)), NZ)
        pltpu.make_async_remote_copy(
            src_ref=sum_mid.at[to],
            dst_ref=sum_in.at[k],
            send_sem=sum_send,
            recv_sem=sum_recv,
            device_id=(to * NC + core, x),
            device_id_type=MESH,
        ).start()
        return carry

    lax.fori_loop(0, CHIPS - 1, send_sum, 0)
    sum_in[CHIPS - 1] = sum_mid[chip]
    all_sums = pltpu.make_async_remote_copy(
        src_ref=sum_mid.at[0 : CHIPS - 1],
        dst_ref=sum_in.at[0 : CHIPS - 1],
        send_sem=sum_send,
        recv_sem=sum_recv,
        device_id=(sibling, x),
        device_id_type=MESH,
    )
    all_sums.wait_recv()
    total = jnp.sum(sum_in[...], axis=0)
    high = jnp.concatenate([total[part * 4 : part * 4 + 4] for part in range(len(SPLIT))], axis=1)
    terms = []
    for _ in range(3):
        term = high.astype(BF).astype(F32)
        terms.append(term)
        high = high - term
    placed = jnp.dot(
        jnp.concatenate(terms, axis=0).astype(BF), back[...], preferred_element_type=F32
    )
    placed = (placed[8:12] + placed[4:8]) + placed[0:4]
    sums, counts = placed[:, 0:COLS], placed[:, PW : PW + COLS]
    book_ref[...] = (sums + ANCHOR * old[...]) / (counts + ANCHOR)

    for swap in swaps:
        swap.wait_send()
    group_copy(LAST, CHIPS_G - 1).wait_send()
    ids_group_copy(LAST, CHIPS_G - 1).wait_send()
    for g in range(LAST):
        group_copy(g, CHIPS_G).wait_send()
        ids_group_copy(g, CHIPS_G).wait_send()
    for copy in [to_right, to_left, on_right, on_left] + shared:
        copy.wait_send()
    for g in range(GROUPS):
        for dt in range(1, NX):
            pay_copy(g, dt).wait_send()
    for part in range(len(SPLIT)):
        pair_copy(part).wait_send()
    all_sums.wait_send()
    for g in range(GROUPS):
        for s in range(NX):
            store_copy(g, s).wait()


def shards(embeddings, coarse_list_index, slots, codes, centroids, rotation, old_codebook):
    spread, back = layout_tables()
    vmem = pl.BlockSpec(memory_space=pltpu.VMEM)
    anywhere = pl.BlockSpec(memory_space=pl.ANY)
    dma = pltpu.SemaphoreType.DMA
    store, book = pl.pallas_call(
        kernel,
        out_shape=(
            jax.ShapeDtypeStruct((COLS, OWNERS * NX * CAP), BF),
            jax.ShapeDtypeStruct((CENT // OWNERS, COLS), F32),
        ),
        in_specs=[anywhere] * 9,
        out_specs=(anywhere, vmem),
        scratch_shapes=[
            pltpu.VMEM((NC * ROW_DEV, MW), BF),
            pltpu.VMEM((NC, 1, ROW_DEV), jnp.int32),
            pltpu.VMEM((NC, 1, ROW_DEV), jnp.int32),
            pltpu.VMEM((NC * ROW_DEV, LANES), jnp.int32),
            pltpu.VMEM((LIST_DEV, D), BF),
            pltpu.VMEM((NX, COLS, D), BF),
            pltpu.VMEM((CENT // OWNERS, COLS), F32),
            pltpu.VMEM((2 * PW, PAY), BF),
            pltpu.VMEM((PW, 2 * PW), BF),
            pltpu.VMEM((GROUPS, CHIPS_G, NC * CAP, MW), BF),
            pltpu.VMEM((GROUPS, CHIPS_G, NC * CAP, MW), BF),
            pltpu.VMEM((GROUPS, 1, LANES), jnp.int32),
            pltpu.VMEM((GROUPS, CHIPS_G, 1, LANES), jnp.int32),
            pltpu.VMEM((ROWS_G, D), BF),
            pltpu.VMEM((LANES, ROWS_G), BF),
            pltpu.VMEM((GROUPS, NX, PAY, ROWS_G), BF),
            pltpu.VMEM((GROUPS, PAY, NX * ROWS_G), BF),
            pltpu.VMEM((SPLIT[0] * OWNERS, NX * ROWS_G), BF),
            pltpu.VMEM((4 * LANES, NX * ROWS_G), BF),
            pltpu.VMEM((len(SPLIT), SPLIT[0] * OWNERS, 4 * LANES), F32),
            pltpu.VMEM((len(SPLIT), NC, CHIPS, 4, LANES), F32),
            pltpu.VMEM((len(SPLIT), CHIPS, 4, LANES), F32),
            pltpu.VMEM((CHIPS, 12, LANES), F32),
            pltpu.VMEM((CHIPS, 12, LANES), F32),
            dma((9,)),
            dma((4,)),
            dma((4,)),
            dma((GROUPS,)),
            dma((GROUPS,)),
            dma((GROUPS,)),
            dma((GROUPS,)),
            dma((7,)),
            dma((7,)),
            dma((GROUPS, NX)),
            dma((GROUPS, NX)),
            dma((1,)),
            dma((len(SPLIT),)),
            dma((len(SPLIT),)),
            dma(()),
            dma(()),
            dma((GROUPS, NX)),
        ],
        compiler_params=pltpu.CompilerParams(
            collective_id=0, has_side_effects=True, vmem_limit_bytes=56 * 2**20
        ),
    )(
        embeddings,
        coarse_list_index.reshape(1, ROW_DEV),
        slots.reshape(1, ROW_DEV),
        codes,
        centroids,
        rotation.T,
        old_codebook,
        jnp.asarray(spread, BF),
        jnp.asarray(back, BF),
    )
    return store.T, book


def solution(mesh):
    return jax.shard_map(
        shards,
        mesh=mesh,
        in_specs=(
            P(("list", "sub"), None),
            P(("list", "sub")),
            P(("list", "sub")),
            P(("list", "sub"), None),
            P("list", None),
            P(None, "sub"),
            P("list", "sub"),
        ),
        out_specs=(P("list", "sub"), P("list", "sub")),
        check_vma=False,
    )
```
